512 devices in a mesh: ty: 32 (over y, x, core), tx: 16 (over z).
Axes of the slice: x: 4, y: 4, z: 16, core: 2. Of those that a mesh axis runs over, the one named last changes fastest.
Arguments:
- features: bfloat16 [9, 1024, 4096], P(None, 'ty', 'tx'), may hold values from -6 to 6
- enc_conv0: bfloat16 [3, 3, 32, 9], replicated, may hold values from -1 to 1
- enc_conv1: bfloat16 [3, 3, 32, 32], replicated, may hold values from -0.5 to 0.5
- enc_conv2: bfloat16 [3, 3, 48, 32], replicated, may hold values from -0.5 to 0.5
- enc_conv3: bfloat16 [3, 3, 64, 48], replicated, may hold values from -0.4375 to 0.4375
- enc_conv4: bfloat16 [3, 3, 80, 64], replicated, may hold values from -0.375 to 0.375
- enc_conv5a: bfloat16 [3, 3, 96, 80], replicated, may hold values from -0.3125 to 0.3125
- enc_conv5b: bfloat16 [3, 3, 96, 96], replicated, may hold values from -0.3125 to 0.3125
- dec_conv4a: bfloat16 [3, 3, 112, 160], replicated, may hold values from -0.21875 to 0.21875
- dec_conv4b: bfloat16 [3, 3, 112, 112], replicated, may hold values from -0.25 to 0.25
- dec_conv3a: bfloat16 [3, 3, 96, 160], replicated, may hold values from -0.21875 to 0.21875
- dec_conv3b: bfloat16 [3, 3, 96, 96], replicated, may hold values from -0.3125 to 0.3125
- dec_conv2a: bfloat16 [3, 3, 64, 128], replicated, may hold values from -0.25 to 0.25
- dec_conv2b: bfloat16 [3, 3, 64, 64], replicated, may hold values from -0.375 to 0.375
- dec_conv1a: bfloat16 [3, 3, 64, 73], replicated, may hold values from -0.3125 to 0.3125
- dec_conv1b: bfloat16 [3, 3, 32, 64], replicated, may hold values from -0.375 to 0.375
- dec_conv0: bfloat16 [3, 3, 3, 32], replicated, may hold values from -0.375 to 0.375
- biases: float32 [1091], replicated, may hold values from -1 to 1
Outputs:
- denoised: bfloat16 [3, 1024, 4096], P(None, 'ty', 'tx')
The draws below stay inside these ranges and needn't reach their ends.
All inputs are finite; a program needn't handle non-finite values.
Results may differ from the reference program's by a relative error of at most 0.038.
Values may be sent and summed in bfloat16 or wider, within the bound.
A program may use at most 64 MiB of HBM per device.

```python
import jax
import jax.numpy as jnp
from jax import lax

CH_IN = 9
CH_E1 = 32
CH_E2 = 48
CH_E3 = 64
CH_E4 = 80
CH_E5 = 96
CH_D4 = 112
CH_D3 = 96
CH_D2 = 64
CH_D1 = 64
CH_D0 = 32
CH_OUT = 3
IMG_H = 1024
IMG_W = 4096
BIAS_COUNT = 1091


def level_of(key, extent, split, smallest, largest):
    gain, own = 1.0, jax.random.fold_in(key, 6)
    for position, parts in split:
        draws = jnp.exp(jax.random.uniform(jax.random.fold_in(own, position), (parts,), jnp.float32, smallest / len(split), largest / len(split)))
        gain = gain * jnp.repeat(draws, extent[position] // parts).reshape([-1 if axis == position else 1 for axis in range(len(extent))])
    return gain


def noise(rng, extent, spread, limit, cuts=(), kind=jnp.bfloat16):
    level = level_of(rng, extent, cuts, -0.22, 0.18) if cuts else 1.0
    entries = jax.random.normal(rng, extent, jnp.float32) * spread * level
    return jnp.minimum(jnp.maximum(entries, -limit), limit).astype(kind)


def setup_inputs(seed: int = 0) -> dict:
    key_list = jax.random.split(jax.random.key(seed), 19)
    features = noise(key_list[0], (CH_IN, IMG_H, IMG_W), 1.0, 6.0, ((1, 32), (2, 16)))
    enc_conv0 = noise(key_list[1], (3, 3, CH_E1, CH_IN), (9 * CH_IN // 2) ** -0.5, 1.0)
    enc_conv1 = noise(key_list[2], (3, 3, CH_E1, CH_E1), (9 * CH_E1 // 2) ** -0.5, 0.5)
    enc_conv2 = noise(key_list[3], (3, 3, CH_E2, CH_E1), (9 * CH_E1 // 2) ** -0.5, 0.5)
    enc_conv3 = noise(key_list[4], (3, 3, CH_E3, CH_E2), (9 * CH_E2 // 2) ** -0.5, 0.4375)
    enc_conv4 = noise(key_list[5], (3, 3, CH_E4, CH_E3), (9 * CH_E3 // 2) ** -0.5, 0.375)
    enc_conv5a = noise(key_list[6], (3, 3, CH_E5, CH_E4), (9 * CH_E4 // 2) ** -0.5, 0.3125)
    enc_conv5b = noise(key_list[7], (3, 3, CH_E5, CH_E5), (9 * CH_E5 // 2) ** -0.5, 0.3125)
    dec_conv4a = noise(key_list[8], (3, 3, CH_D4, CH_E5 + CH_E3), (9 * (CH_E5 + CH_E3) // 2) ** -0.5, 0.21875)
    dec_conv4b = noise(key_list[9], (3, 3, CH_D4, CH_D4), (9 * CH_D4 // 2) ** -0.5, 0.25)
    dec_conv3a = noise(key_list[10], (3, 3, CH_D3, CH_D4 + CH_E2), (9 * (CH_D4 + CH_E2) // 2) ** -0.5, 0.21875)
    dec_conv3b = noise(key_list[11], (3, 3, CH_D3, CH_D3), (9 * CH_D3 // 2) ** -0.5, 0.3125)
    dec_conv2a = noise(key_list[12], (3, 3, CH_D2, CH_D3 + CH_E1), (9 * (CH_D3 + CH_E1) // 2) ** -0.5, 0.25)
    dec_conv2b = noise(key_list[13], (3, 3, CH_D2, CH_D2), (9 * CH_D2 // 2) ** -0.5, 0.375)
    dec_conv1a = noise(key_list[14], (3, 3, CH_D1, CH_D2 + CH_IN), (9 * (CH_D2 + CH_IN) // 2) ** -0.5, 0.3125)
    dec_conv1b = noise(key_list[15], (3, 3, CH_D0, CH_D1), (9 * CH_D1 // 2) ** -0.5, 0.375)
    dec_conv0 = noise(key_list[16], (3, 3, CH_OUT, CH_D0), (9 * CH_D0) ** -0.5, 0.375)
    biases = noise(key_list[17], (BIAS_COUNT,), 0.2, 1.0, (), jnp.float32)
    return dict(features=features, enc_conv0=enc_conv0, enc_conv1=enc_conv1, enc_conv2=enc_conv2, enc_conv3=enc_conv3, enc_conv4=enc_conv4, enc_conv5a=enc_conv5a, enc_conv5b=enc_conv5b, dec_conv4a=dec_conv4a, dec_conv4b=dec_conv4b, dec_conv3a=dec_conv3a, dec_conv3b=dec_conv3b, dec_conv2a=dec_conv2a, dec_conv2b=dec_conv2b, dec_conv1a=dec_conv1a, dec_conv1b=dec_conv1b, dec_conv0=dec_conv0, biases=biases)


def split_biases(biases, weights):
    pieces = []
    offset = 0
    for weight in weights:
        count = weight.shape[2]
        pieces.append(biases[offset:offset + count])
        offset = offset + count
    return pieces


def convolve_whole(field, weight, bias_vec, active):
    channels, height, columns = field.shape
    outputs = weight.shape[2]
    padded = jnp.pad(field, ((0, 0), (1, 1), (1, 1)))
    band_rows = min(height, 64)
    kernel = weight.astype(jnp.float32)

    def one_band(band_index):
        window = lax.dynamic_slice_in_dim(padded, band_index * band_rows, band_rows + 2, 1).astype(jnp.float32)
        summed = jnp.zeros((outputs, band_rows, columns), jnp.float32)
        for row_off in range(3):
            for col_off in range(3):
                summed = summed + jnp.einsum("oc,chw->ohw", kernel[row_off, col_off], window[:, row_off:row_off + band_rows, col_off:col_off + columns], precision=lax.Precision.HIGHEST)
        return summed

    bands = lax.map(one_band, jnp.arange(height // band_rows, dtype=jnp.int32))
    summed = bands.transpose(1, 0, 2, 3).reshape(outputs, height, columns) + bias_vec[:, None, None]
    if active:
        summed = jax.nn.relu(summed)
    return summed.astype(jnp.bfloat16)


def max_pool(field):
    channels, height, columns = field.shape
    return field.reshape(channels, height // 2, 2, columns // 2, 2).max(axis=(2, 4))


def upsample(field):
    channels, height, columns = field.shape
    return jnp.broadcast_to(field[:, :, None, :, None], (channels, height, 2, columns, 2)).reshape(channels, 2 * height, 2 * columns)


def reference(features, enc_conv0, enc_conv1, enc_conv2, enc_conv3, enc_conv4, enc_conv5a, enc_conv5b, dec_conv4a, dec_conv4b, dec_conv3a, dec_conv3b, dec_conv2a, dec_conv2b, dec_conv1a, dec_conv1b, dec_conv0, biases):
    weights = [enc_conv0, enc_conv1, enc_conv2, enc_conv3, enc_conv4, enc_conv5a, enc_conv5b, dec_conv4a, dec_conv4b, dec_conv3a, dec_conv3b, dec_conv2a, dec_conv2b, dec_conv1a, dec_conv1b, dec_conv0]
    shifts = split_biases(biases, weights)

    def layer(number, field):
        return convolve_whole(field, weights[number], shifts[number], number < 15)

    full_res = layer(1, layer(0, features))
    pooled_one = max_pool(full_res)
    half_res = layer(2, pooled_one)
    pooled_two = max_pool(half_res)
    quarter_res = layer(3, pooled_two)
    pooled_three = max_pool(quarter_res)
    eighth_res = layer(4, pooled_three)
    bottom = layer(6, layer(5, max_pool(eighth_res)))
    rise_four = layer(8, layer(7, jnp.concatenate([upsample(bottom), pooled_three], 0)))
    rise_three = layer(10, layer(9, jnp.concatenate([upsample(rise_four), pooled_two], 0)))
    rise_two = layer(12, layer(11, jnp.concatenate([upsample(rise_three), pooled_one], 0)))
    return layer(15, layer(14, layer(13, jnp.concatenate([upsample(rise_two), features], 0))))
```

```python
import functools

import jax
import jax.numpy as jnp
from jax import lax
from jax.experimental import pallas as pl
from jax.experimental.pallas import tpu as pltpu
from jax.sharding import PartitionSpec as P

F32 = jnp.float32
BF = jnp.bfloat16
BIG = 3.0e38
MESH = pl.DeviceIdType.MESH

COUT = [32, 32, 48, 64, 80, 96, 96, 112, 112, 96, 96, 64, 64, 64, 32, 3]
CIN = [9, 32, 32, 48, 64, 80, 96, 160, 112, 160, 96, 128, 64, 73, 64, 32]
NP = [32, 32, 64, 64, 128, 128, 128, 128, 128, 128, 128, 64, 64, 64, 32, 4]
KDIM = [256, 512, 512, 1024, 1024, 2048, 2048, 1536, 2048, 1536, 2048, 1024, 1024, 512, 1024, 512]
DIRS = [(dy, dx) for dy in (-1, 0, 1) for dx in (-1, 0, 1) if (dy, dx) != (0, 0)]
FAR = DIRS + [(dy, dx) for dy in (-3, -2, 2, 3) for dx in (-1, 0, 1)]

SCRATCH = dict(
    rows_in=((2, 9, 32, 256), BF),
    cols_out=((2, 80, 128), BF),
    cols_in=((6, 80, 128), BF),
    tile_out=((64, 128), BF),
    tiles_in=((20, 64, 128), BF),
    ext_side=((9, 96, 128), F32),
    ext=((9, 96, 384), BF),
    spread=((384, 1024), BF),
    planar=((8, 16 * 96, 128), F32),
    rows_yc=((72, 16, 1024), BF),
    eye=((160, 256), BF),
    fwin=((40, 160, 256), BF),
    s1=((36, 160, 256), BF),
    pix1=((34, 176, 128), F32),
    s2=((17, 80, 256), BF),
    pix2=((16, 112, 128), F32),
    s3=((5, 48, 512), BF),
    pix3o=((4, 48, 128), F32),
    pix3=((28, 112, 128), F32),
    s4=((11, 32, 512), BF),
    pix4=((10, 48, 128), F32),
    s5=((5, 16, 1024), BF),
    s6=((4, 16, 1024), BF),
    r7=((6, 32, 256), BF),
    k7=((6, 32, 512), BF),
    s8=((5, 32, 1024), BF),
    r9=((8, 48, 256), BF),
    k9=((8, 48, 512), BF),
    s10=((7, 48, 1024), BF),
    r11=((12, 80, 256), BF),
    k11=((12, 80, 256), BF),
    s12=((11, 80, 512), BF),
    r13=((24, 144, 128), BF),
    s14=((21, 144, 512), BF),
    s15=((20, 144, 256), BF),
    t128=((968, 128), F32),
    t256=((968, 256), F32),
    t512=((360, 512), F32),
    td=((20, 184, 128), F32),
    cap128=((160, 128), F32),
    cap256=((144, 256), F32),
    cap512=((48, 512), F32),
    w15f=((16, 512), F32),
    z0=((144, 144), F32),
    z1=((144, 144), F32),
    zf=((2, 144, 128), F32),
    out32=((6, 32, 128), F32),
)
for _k in range(16):
    SCRATCH["w%d" % _k] = ((16 if _k == 15 else 4 * NP[_k], KDIM[_k]), BF)


def iota(shape, dim):
    return lax.broadcasted_iota(jnp.int32, shape, dim)


def nt(a, b):
    return lax.dot_general(a, b, (((1,), (1,)), ((), ())), preferred_element_type=F32)


def replicated_taps(w, number, first, count, period):
    cin = CIN[number]
    row = iota((cin, 128), 0)
    lane = iota((cin, 128), 1)
    pick = ((row - first == lane % period) & (row >= first) & (row < first + count)).astype(F32).astype(BF)
    return [
        [jnp.dot(w[ky, kx], pick, preferred_element_type=F32) for kx in range(3)] for ky in range(3)
    ]


def choose(groups, period, rows):
    lane = iota((rows, 128), 1)
    value = jnp.zeros((rows, 128), F32)
    for place, tap in enumerate(groups):
        if tap is not None:
            value = jnp.where((lane >= place * period) & (lane < (place + 1) * period), tap, value)
    return value


def tap_of(taps, r, s, qy, qx):
    ky, kx = r - qy, s - qx
    if 0 <= ky < 3 and 0 <= kx < 3:
        return taps[ky][kx]
    return None


def prepare_blocks(wt, w, number, offset, first, count, lanes):
    cout, np_ = COUT[number], NP[number]
    if lanes == 128:
        for ky in range(3):
            for kx in range(3):
                tap = w[ky, kx]
                for qy in range(2):
                    for qx in range(2):
                        r, s = ky + qy, kx + qx
                        t, py, u, px = r // 2, r % 2, s // 2, s % 2
                        k = offset + ((t * 2 + u) * 4 + py * 2 + px) * 128
                        n = (qy * 2 + qx) * np_
                        wt[n : n + cout, k : k + count] = tap
        return
    taps = replicated_taps(w, number, first, count, lanes)
    per = 128 // lanes
    for qy in range(2):
        for qx in range(2):
            n = (qy * 2 + qx) * np_
            for t in range(2):
                for u in range(2):
                    places = [tap_of(taps, 2 * t + py, 2 * u + px, qy, qx) for py in range(2) for px in range(2)]
                    for chunk in range(4 // per):
                        k = offset + (t * 2 + u) * 4 * lanes + chunk * 128
                        value = choose(places[chunk * per : (chunk + 1) * per], lanes, cout)
                        wt[n : n + cout, k : k + 128] = value.astype(BF)


def prepare_window(wt, w, number, offset, first):
    cout, np_ = COUT[number], NP[number]
    taps = replicated_taps(w, number, first, 9, 16)
    for qy in range(2):
        for qx in range(2):
            n = (qy * 2 + qx) * np_
            for half in range(2):
                places = [tap_of(taps, r, s, qy, qx) for s in (2 * half, 2 * half + 1) for r in range(4)]
                value = choose(places, 16, cout)
                wt[n : n + cout, offset + half * 128 : offset + half * 128 + 128] = value.astype(BF)


SUMS = {(0, 0): (0, 1), (0, 1): (2,), (1, 0): (0,), (1, 1): (1, 2)}


def prepare_up(wt, w, number, count, lanes):
    cout, np_ = COUT[number], NP[number]
    if lanes == 128:
        taps = [[w[ky, kx][:, :count].astype(F32) for kx in range(3)] for ky in range(3)]
    else:
        taps = replicated_taps(w, number, 0, count, lanes)
    for qy in range(2):
        for t in range(2):
            for qx in range(2):
                n = (qy * 2 + qx) * np_
                parts = []
                for u in range(2):
                    total = None
                    for ky in SUMS[qy, t]:
                        for kx in SUMS[qx, u]:
                            total = taps[ky][kx] if total is None else total + taps[ky][kx]
                    parts.append(total)
                if lanes == 128:
                    for u in range(2):
                        k = (t * 2 + u) * 128
                        wt[n : n + cout, k : k + count] = parts[u].astype(BF)
                else:
                    wt[n : n + cout, t * 128 : t * 128 + 128] = choose(parts, lanes, cout).astype(BF)


def kernel(sizes, feat, *refs):
    rows_ty, cols_tx = sizes
    weights = refs[:16]
    table = refs[16]
    out = refs[17]
    c = dict(zip(SCRATCH, refs[18 : 18 + len(SCRATCH)]))
    send1, recv1, send2, recv2 = refs[18 + len(SCRATCH) :]
    ty = lax.axis_index("ty")
    tx = lax.axis_index("tx")

    def device(dy, dx):
        return (lax.rem(ty + dy + rows_ty, rows_ty), lax.rem(tx + dx + cols_tx, cols_tx))

    barrier = pltpu.get_barrier_semaphore()
    for dy, dx in FAR:
        pl.semaphore_signal(barrier, inc=1, device_id=device(dy, dx), device_id_type=MESH)

    lane9 = iota((9, 8, 128), 2)
    for side in range(2):
        value = jnp.zeros((9, 8, 128), F32)
        for g in range(4):
            piece = feat[:, 8 * g : 8 * g + 8, 128 * side : 128 * side + 128].astype(F32)
            shift = (32 * g - 96 * side) % 128
            if shift:
                piece = pltpu.roll(piece, shift, 2)
            value = jnp.where((lane9 >= 32 * g) & (lane9 < 32 * g + 32), piece, value)
        c["cols_out"][side, 0:72, :] = value.reshape(72, 128).astype(BF)
        c["cols_out"][side, 64:80, :] = jnp.concatenate(
            [value.reshape(72, 128)[64:72], jnp.zeros((8, 128), F32)], 0
        ).astype(BF)

    pl.semaphore_wait(barrier, len(FAR))
    copies = []
    for number, (dy, dx) in enumerate(DIRS):
        if dx == 0:
            source, target = feat, c["rows_in"].at[0 if dy == 1 else 1]
        else:
            source = c["cols_out"].at[0 if dx == -1 else 1]
            target = c["cols_in"].at[(0 if dx == -1 else 3) + dy + 1]
        copy = pltpu.make_async_remote_copy(
            src_ref=source,
            dst_ref=target,
            send_sem=send1.at[number],
            recv_sem=recv1.at[number],
            device_id=device(dy, dx),
            device_id_type=MESH,
        )
        copy.start()
        copies.append(copy)

    for number in (2, 4, 5, 6, 7, 8, 9, 10):
        c["w%d" % number][...] = jnp.zeros(c["w%d" % number].shape, BF)
    prepare_window(c["w0"], weights[0], 0, 0, 0)
    prepare_blocks(c["w1"], weights[1], 1, 0, 0, 32, 32)
    prepare_blocks(c["w2"], weights[2], 2, 0, 0, 32, 32)
    prepare_blocks(c["w3"], weights[3], 3, 0, 0, 48, 64)

    place = iota((384, 1024), 0)
    target = iota((384, 1024), 1)
    x = jnp.where(place < 256, place, jnp.where(place < 288, place - 288, jnp.where(place < 320, place - 32, -1000)))
    want = 2 * (target % 256) + target // 256 - 36
    c["spread"][...] = (x == want).astype(F32).astype(BF)
    c["eye"][...] = (iota((160, 256), 0) == iota((160, 256), 1)).astype(F32).astype(BF)
    for k in range(8):
        c["planar"][k, 864:1536, :] = jnp.zeros((672, 128), F32)

    for copy in copies:
        copy.wait()

    first_row = jnp.where(ty > 0, 1.0, 0.0)
    last_row = jnp.where(ty < rows_ty - 1, 1.0, 0.0)
    first_col = jnp.where(tx > 0, 1.0, 0.0)
    last_col = jnp.where(tx < cols_tx - 1, 1.0, 0.0)
    c["ext"][:, 0:32, 0:256] = jnp.where(first_row > 0, c["rows_in"][0].astype(F32), 0.0).astype(BF)
    c["ext"][:, 32:64, 0:256] = feat[...]
    c["ext"][:, 64:96, 0:256] = jnp.where(last_row > 0, c["rows_in"][1].astype(F32), 0.0).astype(BF)
    for k in range(3):
        row_ok = (first_row, 1.0, last_row)[k]
        left = c["cols_in"][3 + (1, 0, -1)[k] + 1].astype(F32)[0:72].reshape(9, 8, 128)
        right = c["cols_in"][(1, 0, -1)[k] + 1].astype(F32)[0:72].reshape(9, 8, 128)
        left = jnp.where(row_ok * first_col > 0, left, 0.0)
        right = jnp.where(row_ok * last_col > 0, right, 0.0)
        for g in range(4):
            to_left = pltpu.roll(left, (128 - 32 * g) % 128, 2) if g else left
            to_right = pltpu.roll(right, (160 - 32 * g) % 128, 2) if g != 1 else right
            piece = jnp.where(lane9 < 32, to_left, jnp.where(lane9 < 64, to_right, 0.0))
            c["ext_side"][:, 32 * k + 8 * g : 32 * k + 8 * g + 8, :] = piece
    c["ext"][:, :, 256:384] = c["ext_side"][...].astype(BF)

    def spread_channel(ch, _):
        wide = jnp.dot(c["ext"][ch], c["spread"][...], preferred_element_type=F32)
        for k in range(8):
            c["planar"][k, pl.ds(pl.multiple_of(ch * 96, 96), 96), :] = wide[:, 128 * k : 128 * k + 128]
        return 0

    lax.fori_loop(0, 9, spread_channel, 0)

    def gather_row(y, _):
        for k in range(8):
            c["rows_yc"][y, :, 128 * k : 128 * k + 128] = c["planar"][k, pl.ds(y + 12, 16, stride=96), :].astype(BF)
        return 0

    lax.fori_loop(0, 72, gather_row, 0)

    def column_caps(number, wp, origin, width):
        np_ = NP[number]
        n = 4 * np_
        cap = c["cap%d" % n]
        at = origin + 2 * iota((wp, n), 0) + (iota((wp, n), 1) // np_) % 2 + tx * width
        cap[0:wp, :] = jnp.where((at >= 0) & (at < width * cols_tx), BIG, 0.0)
        return cap

    def finish(number, r, cap, i0, g, wp, origin, height):
        np_ = NP[number]
        n = 4 * np_
        u = jnp.maximum(r + table[number : number + 1, 0:n], 0.0)
        pieces = []
        for k in range(g):
            at = origin + 2 * (i0 + k) + iota((1, n), 1) // (2 * np_) + ty * height
            row = jnp.where((at >= 0) & (at < height * rows_ty), BIG, 0.0)
            pieces.append(jnp.minimum(u[k * wp : (k + 1) * wp], jnp.minimum(cap[0:wp, :], row)))
        return pieces

    def to_blocks(pieces, target, i0, wp, n):
        t = c["t%d" % n]
        g = len(pieces)
        for k in range(g):
            t[k * wp : (k + 1) * wp, :] = pieces[k]
            target[i0 + k, :, 0:n] = pieces[k].astype(BF)
        for k in range(g):
            target[i0 + k, :, n : 2 * n] = t[k * wp + 1 : (k + 1) * wp + 1, :].astype(BF)

    def pooled(piece, np_):
        if np_ == 32:
            m = jnp.maximum(piece, pltpu.roll(piece, 64, 1))
            return jnp.maximum(m, pltpu.roll(m, 32, 1))
        if np_ == 64:
            m = jnp.maximum(piece[:, 0:128], piece[:, 128:256])
            return jnp.maximum(m, pltpu.roll(m, 64, 1))
        m = jnp.maximum(piece[:, 0:128], piece[:, 128:256])
        return jnp.maximum(m, jnp.maximum(piece[:, 256:384], piece[:, 384:512]))

    def pack(pixels, target, count, wp, lanes, row0, col0):
        lane = iota((wp, 128), 1)

        def step(i, _):
            a = [
                [pixels[row0 + 2 * i + py, pl.ds(col0 + m, wp, stride=2), :] for m in range(4)] for py in range(2)
            ]
            for u in range(2):
                four = [a[0][2 * u], a[0][2 * u + 1], a[1][2 * u], a[1][2 * u + 1]]
                base = u * 4 * lanes
                if lanes == 32:
                    v = jnp.where(
                        lane < 64,
                        jnp.where(lane < 32, four[0], four[1]),
                        jnp.where(lane < 96, four[2], four[3]),
                    )
                    target[i, :, base : base + 128] = v.astype(BF)
                elif lanes == 64:
                    for py in range(2):
                        v = jnp.where(lane < 64, four[2 * py], four[2 * py + 1])
                        target[i, :, base + 128 * py : base + 128 * py + 128] = v.astype(BF)
                else:
                    for q in range(4):
                        target[i, :, base + 128 * q : base + 128 * q + 128] = four[q].astype(BF)
            return 0

        lax.fori_loop(0, count, step, 0)

    def to_pixels(pieces, target, i0, wp, wr, np_):
        td = c["td"]
        lane = iota((wp, 128), 1)
        lane_r = iota((wr, 128), 1)
        for k in range(len(pieces)):
            for qy in range(2):
                at = 2 * k + qy
                if np_ == 128:
                    even = pieces[k][:, 256 * qy : 256 * qy + 128]
                    odd = pieces[k][:, 256 * qy + 128 : 256 * qy + 256]
                else:
                    v = pieces[k][:, 128 * qy : 128 * qy + 128]
                    w = pltpu.roll(v, 64, 1)
                    even = jnp.where(lane < 64, v, w)
                    odd = jnp.where(lane < 64, w, v)
                td[at, pl.ds(0, wp, stride=2), :] = even
                td[at, pl.ds(1, wp, stride=2), :] = odd
        for k in range(len(pieces)):
            for qy in range(2):
                at = 2 * k + qy
                here, right = td[at, 0:wr, :], td[at, 1 : wr + 1, :]
                if np_ == 128:
                    target[2 * (i0 + k) + qy, :, 0:128] = here.astype(BF)
                    target[2 * (i0 + k) + qy, :, 128:256] = right.astype(BF)
                else:
                    target[2 * (i0 + k) + qy, :, :] = jnp.where(lane_r < 64, here, right).astype(BF)

    def block_input(ref):
        def load(i0, g):
            lanes = ref.shape[2]
            rows = g * ref.shape[1]
            return [
                ref[pl.ds(i0, g)].reshape(rows, lanes),
                ref[pl.ds(i0 + 1, g)].reshape(rows, lanes),
            ]

        return load

    def layer(number, loads, count, g, wp, origin_y, origin_x, level, store):
        height, width = 32 >> level, 256 >> level
        cap = column_caps(number, wp, origin_x, width)

        def step(it, _):
            i0 = it * g
            lhs = []
            for load in loads:
                lhs = lhs + load(i0, g)
            lhs = jnp.concatenate(lhs, axis=1) if len(lhs) > 1 else lhs[0]
            r = nt(lhs, c["w%d" % number][...])
            store(finish(number, r, cap, i0, g, wp, origin_y, height), i0)
            return 0

        if count == 1:
            step(0, 0)
        else:
            lax.fori_loop(0, count, step, 0)

    def pool_into(pixels, number, wp):
        def store(pieces, i0):
            for k, piece in enumerate(pieces):
                pixels[i0 + k, 0:wp, :] = pooled(piece, NP[number])

        return store

    def windows(i, _):
        rows = c["rows_yc"][pl.ds(2 * i, 4)].reshape(64, 1024)
        stacked = jnp.concatenate([rows[:, 256 * s : 256 * s + 256] for s in range(4)], axis=0)
        c["fwin"][i] = nt(c["eye"][...], stacked).astype(BF)
        return 0

    lax.fori_loop(0, 35, windows, 0)

    def window_load(i0, g):
        return [c["fwin"][pl.ds(i0, g)].reshape(g * 160, 256)]

    layer(0, [window_load], 7, 5, 160, -19, -35, 0, lambda p, i0: to_blocks(p, c["s1"], i0, 160, 128))
    layer(1, [block_input(c["s1"])], 17, 2, 160, -18, -34, 0, pool_into(c["pix1"], 1, 160))
    pack(c["pix1"], c["s2"], 17, 80, 32, 0, 8)
    layer(2, [block_input(c["s2"])], 4, 4, 80, -8, -8, 1, pool_into(c["pix2"], 2, 80))
    pack(c["pix2"], c["s3"], 5, 48, 64, 3, 3)
    layer(3, [block_input(c["s3"])], 1, 4, 48, 0, 0, 2, pool_into(c["pix3o"], 3, 48))

    lane16 = iota((16, 128), 1)
    for y in range(4):
        even = c["pix3o"][y, pl.ds(0, 16, stride=2), :]
        odd = c["pix3o"][y, pl.ds(1, 16, stride=2), :]
        c["tile_out"][16 * y : 16 * y + 16, :] = jnp.where(lane16 < 64, even, odd).astype(BF)
    copies = []
    for number, (dy, dx) in enumerate(FAR):
        copy = pltpu.make_async_remote_copy(
            src_ref=c["tile_out"],
            dst_ref=c["tiles_in"].at[number],
            send_sem=send2.at[number],
            recv_sem=recv2.at[number],
            device_id=device(dy, dx),
            device_id_type=MESH,
        )
        copy.start()
        copies.append(copy)

    prepare_blocks(c["w4"], weights[4], 4, 0, 0, 64, 64)
    prepare_blocks(c["w5"], weights[5], 5, 0, 0, 80, 128)
    prepare_blocks(c["w6"], weights[6], 6, 0, 0, 96, 128)
    prepare_up(c["w7"], weights[7], 7, 96, 128)
    prepare_blocks(c["w7"], weights[7], 7, 512, 96, 64, 64)
    prepare_blocks(c["w8"], weights[8], 8, 0, 0, 112, 128)
    prepare_up(c["w9"], weights[9], 9, 112, 128)
    prepare_blocks(c["w9"], weights[9], 9, 512, 112, 48, 64)
    prepare_blocks(c["w10"], weights[10], 10, 0, 0, 96, 128)
    prepare_blocks(c["w12"], weights[12], 12, 0, 0, 64, 64)
    prepare_up(c["w13"], weights[13], 13, 64, 64)
    prepare_window(c["w13"], weights[13], 13, 256, 64)
    prepare_blocks(c["w14"], weights[14], 14, 0, 0, 64, 64)
    c["w11"][...] = jnp.zeros(c["w11"].shape, BF)
    prepare_up(c["w11"], weights[11], 11, 96, 128)
    prepare_blocks(c["w11"], weights[11], 11, 512, 96, 32, 32)
    taps = replicated_taps(weights[15], 15, 0, 32, 32)
    c["w15f"][...] = jnp.zeros((16, 512), F32)
    for qx in range(2):
        for qy in range(2):
            n = qx * 8 + qy * 3
            for t in range(2):
                for u in range(2):
                    places = [tap_of(taps, 2 * t + py, 2 * u + px, qy, qx) for py in range(2) for px in range(2)]
                    k = (t * 2 + u) * 128
                    c["w15f"][n : n + 3, k : k + 128] = choose(places, 32, 3)
    c["w15"][...] = c["w15f"][...].astype(BF)
    pack(c["pix1"], c["k11"], 12, 80, 32, 5, 13)
    pack(c["pix2"], c["k9"], 8, 48, 64, 0, 0)

    for copy in copies:
        copy.wait()

    slot = {d: n for n, d in enumerate(FAR)}
    for ky in range(-3, 4):
        for kx in range(-1, 2):
            if (ky, kx) == (0, 0):
                tile = c["tile_out"][...].astype(F32)
            else:
                ok = (ty + ky >= 0) & (ty + ky < rows_ty) & (tx + kx >= 0) & (tx + kx < cols_tx)
                tile = jnp.where(jnp.where(ok, 1.0, 0.0) > 0, c["tiles_in"][slot[-ky, -kx]].astype(F32), 0.0)
            for y in range(4):
                if ky == -3 and y < 3 or ky == 3 and y > 0:
                    continue
                v = tile[16 * y : 16 * y + 16]
                w = pltpu.roll(v, 64, 1)
                row = 12 + 4 * ky + y
                col = 32 * (kx + 1)
                c["pix3"][row, pl.ds(col, 16, stride=2), :] = jnp.where(lane16 < 64, v, w)
                c["pix3"][row, pl.ds(col + 1, 16, stride=2), :] = jnp.where(lane16 < 64, w, v)

    pack(c["pix3"], c["s4"], 11, 32, 64, 3, 23)
    pack(c["pix3"], c["k7"], 6, 32, 64, 8, 28)

    layer(4, [block_input(c["s4"])], 2, 5, 32, -8, -8, 3, pool_into(c["pix4"], 4, 32))
    pack(c["pix4"], c["s5"], 5, 16, 128, 0, 0)
    layer(5, [block_input(c["s5"])], 1, 4, 16, -3, -3, 4, lambda p, i0: to_blocks(p, c["s6"], i0, 16, 512))
    layer(6, [block_input(c["s6"])], 1, 3, 16, -2, -2, 4, lambda p, i0: to_pixels(p, c["r7"], i0, 16, 32, 128))
    layer(
        7, [block_input(c["r7"]), block_input(c["k7"])], 1, 5, 32, -3, -3, 3,
        lambda p, i0: to_blocks(p, c["s8"], i0, 32, 512),
    )
    layer(8, [block_input(c["s8"])], 1, 4, 32, -2, -2, 3, lambda p, i0: to_pixels(p, c["r9"], i0, 32, 48, 128))
    layer(
        9, [block_input(c["r9"]), block_input(c["k9"])], 1, 7, 48, -3, -3, 2,
        lambda p, i0: to_blocks(p, c["s10"], i0, 48, 512),
    )
    layer(10, [block_input(c["s10"])], 1, 6, 48, -2, -2, 2, lambda p, i0: to_pixels(p, c["r11"], i0, 48, 80, 128))
    layer(
        11, [block_input(c["r11"]), block_input(c["k11"])], 1, 11, 80, -3, -3, 1,
        lambda p, i0: to_blocks(p, c["s12"], i0, 80, 256),
    )
    layer(12, [block_input(c["s12"])], 2, 5, 80, -2, -2, 1, lambda p, i0: to_pixels(p, c["r13"], i0, 80, 144, 64))

    def features_load(i0, g):
        return [c["fwin"][pl.ds(i0 + 8, g), 16:160, :].reshape(g * 144, 256)]

    layer(
        13, [block_input(c["r13"]), features_load], 5, 4, 144, -3, -3, 0,
        lambda p, i0: to_blocks(p, c["s14"], i0, 144, 256),
    )
    layer(14, [block_input(c["s14"])], 6, 3, 144, -2, -2, 0, lambda p, i0: to_blocks(p, c["s15"], i0, 144, 128))

    lane144 = iota((16, 144), 1)

    def last(i, _):
        field = jnp.concatenate([c["s15"][i], c["s15"][i + 1]], axis=1)
        r = nt(c["w15"][...], field) + table[16:32, 0:144]
        r = jnp.where(lane144 < 129, r, 0.0)
        c["z0"][pl.ds(pl.multiple_of(8 * i, 8), 8), :] = r[0:8]
        c["z1"][pl.ds(pl.multiple_of(8 * i, 8), 8), :] = r[8:16]
        return 0

    c["z0"][136:144, :] = jnp.zeros((8, 144), F32)
    c["z1"][136:144, :] = jnp.zeros((8, 144), F32)
    lax.fori_loop(0, 17, last, 0)
    at = iota((144, 256), 1) - 2 * iota((144, 256), 0)
    even = (at == -1).astype(F32).astype(BF)
    odd = (at == 0).astype(F32).astype(BF)
    wide = jnp.dot(c["z0"][...].astype(BF), even, preferred_element_type=F32) + jnp.dot(
        c["z1"][...].astype(BF), odd, preferred_element_type=F32
    )
    for half in range(2):
        lanes = slice(128 * half, 128 * half + 128)
        c["zf"][half] = wide[:, lanes]
        for o in range(3):
            c["out32"][2 * o + half, pl.ds(0, 16, stride=2), :] = c["zf"][half, pl.ds(3 + o, 16, stride=8), :]
            c["out32"][2 * o + half, pl.ds(1, 16, stride=2), :] = c["zf"][half, pl.ds(8 + o, 16, stride=8), :]
            out[o, :, lanes] = c["out32"][2 * o + half].astype(BF)


def bias_table(biases):
    rows = []
    offset = 0
    for number in range(16):
        piece = biases[offset : offset + COUT[number]]
        offset = offset + COUT[number]
        if number == 15:
            six = jnp.concatenate([piece, piece, jnp.zeros((2,), F32)])
            column = jnp.concatenate([six, six])
            rows.append(jnp.zeros((1, 512), F32))
            rows.append(jnp.broadcast_to(column[:, None], (16, 512)))
        else:
            phase = jnp.pad(piece, (0, NP[number] - COUT[number]))
            four = jnp.concatenate([phase] * 4)
            rows.append(jnp.pad(four, (0, 512 - 4 * NP[number]))[None])
    return jnp.concatenate(rows, axis=0)


def body(sizes, features, *rest):
    weights, biases = rest[:16], rest[16]
    vmem = pl.BlockSpec(memory_space=pltpu.VMEM)
    scratch = [pltpu.VMEM(shape, kind) for shape, kind in SCRATCH.values()]
    scratch += [pltpu.SemaphoreType.DMA((n,)) for n in (8, 8, 20, 20)]
    return pl.pallas_call(
        functools.partial(kernel, sizes),
        out_shape=jax.ShapeDtypeStruct((3, 32, 256), BF),
        in_specs=[vmem] * 18,
        out_specs=vmem,
        scratch_shapes=scratch,
        compiler_params=pltpu.CompilerParams(
            collective_id=0, has_side_effects=True, vmem_limit_bytes=58 << 20
        ),
    )(features, *weights, bias_table(biases))


def solution(mesh):
    sizes = (mesh.shape["ty"], mesh.shape["tx"])
    return jax.shard_map(
        functools.partial(body, sizes),
        mesh=mesh,
        in_specs=(P(None, "ty", "tx"),) + (P(),) * 17,
        out_specs=P(None, "ty", "tx"),
        check_vma=False,
    )
```

```python
import functools

import jax
import jax.numpy as jnp
from jax import lax
from jax.experimental import pallas as pl
from jax.experimental.pallas import tpu as pltpu
from jax.sharding import PartitionSpec as P

F32 = jnp.float32
BF = jnp.bfloat16
BIG = 3.0e38
MESH = pl.DeviceIdType.MESH

COUT = [32, 32, 48, 64, 80, 96, 96, 112, 112, 96, 96, 64, 64, 64, 32, 3]
CIN = [9, 32, 32, 48, 64, 80, 96, 160, 112, 160, 96, 128, 64, 73, 64, 32]
NP = [32, 32, 64, 64, 128, 128, 128, 128, 128, 128, 128, 64, 64, 64, 32, 4]
KDIM = [256, 512, 512, 1024, 1024, 2048, 2048, 1536, 2048, 1536, 2048, 1024, 1024, 512, 1024, 512]
DIRS = [(dy, dx) for dy in (-1, 0, 1) for dx in (-1, 0, 1) if (dy, dx) != (0, 0)]
FAR = DIRS + [(dy, dx) for dy in (-3, -2, 2, 3) for dx in (-1, 0, 1)]

SCRATCH = dict(
    rows_in=((2, 9, 32, 256), BF),
    cols_out=((2, 80, 128), BF),
    cols_in=((6, 80, 128), BF),
    tile_out=((64, 128), BF),
    tiles_in=((20, 64, 128), BF),
    ext_side=((9, 96, 128), F32),
    ext=((9, 96, 384), BF),
    spread=((384, 512), BF),
    planar=((4, 16 * 96, 128), F32),
    rows_yc=((72, 16, 512), BF),
    eye=((160, 256), BF),
    fwin=((40, 160, 256), BF),
    s1=((36, 160, 256), BF),
    pix1=((34, 176, 128), F32),
    s2=((17, 80, 256), BF),
    pix2=((16, 112, 128), F32),
    s3=((5, 48, 512), BF),
    pix3o=((4, 48, 128), F32),
    pix3=((28, 112, 128), F32),
    s4=((11, 32, 512), BF),
    pix4=((10, 48, 128), F32),
    s5=((5, 16, 1024), BF),
    s6=((4, 16, 1024), BF),
    r7=((6, 32, 256), BF),
    k7=((6, 32, 512), BF),
    s8=((5, 32, 1024), BF),
    r9=((8, 48, 256), BF),
    k9=((8, 48, 512), BF),
    s10=((7, 48, 1024), BF),
    r11=((12, 80, 256), BF),
    k11=((12, 80, 256), BF),
    s12=((11, 80, 512), BF),
    r13=((24, 144, 128), BF),
    s14=((21, 144, 512), BF),
    s15=((20, 144, 256), BF),
    t128=((1928, 128), F32),
    t256=((1448, 256), F32),
    t512=((360, 512), F32),
    td=((20, 184, 128), F32),
    cap128=((160, 128), F32),
    cap256=((144, 256), F32),
    cap512=((48, 512), F32),
    w15f=((16, 512), F32),
    flat=((16, 128), F32),
    table=((16, 512), F32),
    column=((16, 144), F32),
    z0=((144, 144), F32),
    z1=((144, 144), F32),
    zf=((2, 144, 128), F32),
    out32=((6, 32, 128), F32),
)
for _k in range(16):
    _n = 16 if _k == 15 else 4 * NP[_k]
    SCRATCH["w%d" % _k] = ((KDIM[_k], _n) if _k in (0, 2, 3, 4, 5, 7, 9) else (_n, KDIM[_k]), BF)


def iota(shape, dim):
    return lax.broadcasted_iota(jnp.int32, shape, dim)


def nt(a, b):
    return lax.dot_general(a, b, (((1,), (1,)), ((), ())), preferred_element_type=F32)


FLIPPED = (0, 2, 3, 4, 5, 7, 9)


def tap_of(w, number, ky, kx, first, count):
    if number == 0:
        return w[ky, :, kx, :]
    if number in FLIPPED:
        return w[ky, kx, first : first + count, :]
    return w[ky, kx][:, first : first + count]


def put(wt, number, n, k, tap):
    if number in FLIPPED:
        wt[k : k + tap.shape[0], n : n + tap.shape[1]] = tap
    else:
        wt[n : n + tap.shape[0], k : k + tap.shape[1]] = tap


def prepare_blocks(wt, w, number, offset, first, count, lanes):
    for ky in range(3):
        for kx in range(3):
            tap = tap_of(w, number, ky, kx, first, count)
            for qy in range(2):
                for qx in range(2):
                    r, s = ky + qy, kx + qx
                    k = offset + ((r // 2 * 2 + s // 2) * 4 + r % 2 * 2 + s % 2) * lanes
                    put(wt, number, (qy * 2 + qx) * NP[number], k, tap)


def prepare_window(wt, w, number, offset, first):
    for ky in range(3):
        for kx in range(3):
            tap = tap_of(w, number, ky, kx, first, 9)
            for qy in range(2):
                for qx in range(2):
                    k = offset + (kx + qx) * 64 + (ky + qy) * 16
                    put(wt, number, (qy * 2 + qx) * NP[number], k, tap)


SUMS = {(0, 0): (0, 1), (0, 1): (2,), (1, 0): (0,), (1, 1): (1, 2)}


def prepare_up(wt, w, number, count, lanes):
    taps = [[tap_of(w, number, ky, kx, 0, count).astype(F32) for kx in range(3)] for ky in range(3)]
    for qy in range(2):
        for t in range(2):
            rows = SUMS[qy, t]
            line = taps[rows[0]] if len(rows) == 1 else [taps[rows[0]][kx] + taps[rows[1]][kx] for kx in range(3)]
            for qx in range(2):
                for u in range(2):
                    cols = SUMS[qx, u]
                    total = line[cols[0]] if len(cols) == 1 else line[cols[0]] + line[cols[1]]
                    put(wt, number, (qy * 2 + qx) * NP[number], (t * 2 + u) * lanes, total.astype(BF))


def prepare_biases(biases, flat, table, column):
    flat[...] = jnp.zeros(flat.shape, F32)
    for r in range(8):
        flat[r : r + 1, :] = biases[pl.ds(128 * r, 128)].reshape(1, 128)
    flat[8:9, 0:67] = biases[pl.ds(1024, 67)].reshape(1, 67)
    lane = iota((8, 128), 1)
    offset = 0
    for number in range(16):
        r, m = offset // 128, offset % 128
        offset = offset + COUT[number]
        pair = jnp.concatenate([flat[r : r + 1, :], flat[r + 1 : r + 2, :]], axis=1)
        pair = jnp.broadcast_to(pair, (8, 256))
        if m:
            pair = pltpu.roll(pair, 256 - m, 1)
        value = jnp.where(lane < COUT[number], pair[:, 0:128], 0.0)
        if number == 15:
            row = iota((16, 128), 0) % 8
            twice = jnp.concatenate([value, value], axis=0)
            mine = jnp.where((iota((16, 128), 1) == row % 3) & (row < 6), twice, 0.0)
            column[...] = jnp.broadcast_to(jnp.sum(mine, axis=1, keepdims=True), (16, 144))
            continue
        if NP[number] == 32:
            value = value + pltpu.roll(value, 32, 1)
        if NP[number] <= 64:
            value = value + pltpu.roll(value, 64, 1)
        for k in range(4 * NP[number] // 128):
            table[number : number + 1, 128 * k : 128 * k + 128] = value[0:1]


def kernel(sizes, feat, *refs):
    rows_ty, cols_tx = sizes
    weights = refs[:16]
    out = refs[17]
    c = dict(zip(SCRATCH, refs[18 : 18 + len(SCRATCH)]))
    send1, recv1, send2, recv2 = refs[18 + len(SCRATCH) :]
    table = c["table"]
    ty = lax.axis_index("ty")
    tx = lax.axis_index("tx")

    def device(dy, dx):
        return (lax.rem(ty + dy + rows_ty, rows_ty), lax.rem(tx + dx + cols_tx, cols_tx))

    barrier = pltpu.get_barrier_semaphore()
    for dy, dx in FAR:
        pl.semaphore_signal(barrier, inc=1, device_id=device(dy, dx), device_id_type=MESH)

    lane9 = iota((9, 8, 128), 2)
    for side in range(2):
        value = jnp.zeros((9, 8, 128), F32)
        for g in range(4):
            piece = feat[:, 8 * g : 8 * g + 8, 128 * side : 128 * side + 128].astype(F32)
            shift = (32 * g - 96 * side) % 128
            if shift:
                piece = pltpu.roll(piece, shift, 2)
            value = jnp.where((lane9 >= 32 * g) & (lane9 < 32 * g + 32), piece, value)
        c["cols_out"][side, 0:72, :] = value.reshape(72, 128).astype(BF)
        c["cols_out"][side, 64:80, :] = jnp.concatenate(
            [value.reshape(72, 128)[64:72], jnp.zeros((8, 128), F32)], 0
        ).astype(BF)

    def clear(number):
        c["w%d" % number][...] = jnp.zeros(c["w%d" % number].shape, BF)

    for number in range(4):
        clear(number)
    prepare_window(c["w0"], weights[0], 0, 0, 0)
    prepare_blocks(c["w1"], weights[1], 1, 0, 0, 32, 32)
    prepare_blocks(c["w2"], weights[2], 2, 0, 0, 32, 32)
    prepare_blocks(c["w3"], weights[3], 3, 0, 0, 48, 64)
    prepare_biases(refs[16], c["flat"], c["table"], c["column"])

    place = iota((384, 128), 0)
    x = jnp.where(place < 256, place, jnp.where(place < 288, place - 288, jnp.where(place < 320, place - 32, -1000)))
    x = x - 2 * iota((384, 128), 1) + 36
    for px in range(2):
        for half in range(2):
            hit = jnp.where(x == px + 256 * half, 1.0, 0.0)
            c["spread"][:, 256 * px + 128 * half : 256 * px + 128 * half + 128] = hit.astype(BF)
    c["eye"][...] = (iota((160, 256), 0) == iota((160, 256), 1)).astype(F32).astype(BF)
    for k in range(4):
        c["planar"][k, 864:1536, :] = jnp.zeros((672, 128), F32)

    pl.semaphore_wait(barrier, len(FAR))
    copies = []
    for number, (dy, dx) in enumerate(DIRS):
        if dx == 0:
            source, target = feat, c["rows_in"].at[0 if dy == 1 else 1]
        else:
            source = c["cols_out"].at[0 if dx == -1 else 1]
            target = c["cols_in"].at[(0 if dx == -1 else 3) + dy + 1]
        copy = pltpu.make_async_remote_copy(
            src_ref=source,
            dst_ref=target,
            send_sem=send1.at[number],
            recv_sem=recv1.at[number],
            device_id=device(dy, dx),
            device_id_type=MESH,
        )
        copy.start()
        copies.append(copy)

    for number in range(4, 15):
        clear(number)
    prepare_blocks(c["w4"], weights[4], 4, 0, 0, 64, 64)
    prepare_blocks(c["w5"], weights[5], 5, 0, 0, 80, 128)
    prepare_blocks(c["w6"], weights[6], 6, 0, 0, 96, 128)
    prepare_up(c["w7"], weights[7], 7, 96, 128)
    prepare_blocks(c["w7"], weights[7], 7, 512, 96, 64, 64)
    prepare_blocks(c["w8"], weights[8], 8, 0, 0, 112, 128)
    prepare_up(c["w9"], weights[9], 9, 112, 128)
    prepare_blocks(c["w9"], weights[9], 9, 512, 112, 48, 64)
    prepare_blocks(c["w10"], weights[10], 10, 0, 0, 96, 128)
    prepare_up(c["w11"], weights[11], 11, 96, 128)
    prepare_blocks(c["w11"], weights[11], 11, 512, 96, 32, 32)
    prepare_blocks(c["w12"], weights[12], 12, 0, 0, 64, 64)
    prepare_up(c["w13"], weights[13], 13, 64, 64)
    prepare_window(c["w13"], weights[13], 13, 256, 64)
    prepare_blocks(c["w14"], weights[14], 14, 0, 0, 64, 64)
    c["w15f"][...] = jnp.zeros((16, 512), F32)
    for ky in range(3):
        for kx in range(3):
            tap = weights[15][ky, kx].astype(F32)
            for qy in range(2):
                for qx in range(2):
                    r, s = ky + qy, kx + qx
                    k = ((r // 2 * 2 + s // 2) * 4 + r % 2 * 2 + s % 2) * 32
                    n = qx * 8 + qy * 3
                    c["w15f"][n : n + 3, k : k + 32] = tap
    c["w15"][...] = c["w15f"][...].astype(BF)
    for copy in copies:
        copy.wait()

    first_row = jnp.where(ty > 0, 1.0, 0.0)
    last_row = jnp.where(ty < rows_ty - 1, 1.0, 0.0)
    first_col = jnp.where(tx > 0, 1.0, 0.0)
    last_col = jnp.where(tx < cols_tx - 1, 1.0, 0.0)
    c["ext"][:, 0:32, 0:256] = jnp.where(first_row > 0, c["rows_in"][0].astype(F32), 0.0).astype(BF)
    c["ext"][:, 32:64, 0:256] = feat[...]
    c["ext"][:, 64:96, 0:256] = jnp.where(last_row > 0, c["rows_in"][1].astype(F32), 0.0).astype(BF)
    for k in range(3):
        row_ok = (first_row, 1.0, last_row)[k]
        left = c["cols_in"][3 + (1, 0, -1)[k] + 1].astype(F32)[0:72].reshape(9, 8, 128)
        right = c["cols_in"][(1, 0, -1)[k] + 1].astype(F32)[0:72].reshape(9, 8, 128)
        left = jnp.where(row_ok * first_col > 0, left, 0.0)
        right = jnp.where(row_ok * last_col > 0, right, 0.0)
        for g in range(4):
            to_left = pltpu.roll(left, (128 - 32 * g) % 128, 2) if g else left
            to_right = pltpu.roll(right, (160 - 32 * g) % 128, 2) if g != 1 else right
            piece = jnp.where(lane9 < 32, to_left, jnp.where(lane9 < 64, to_right, 0.0))
            c["ext_side"][:, 32 * k + 8 * g : 32 * k + 8 * g + 8, :] = piece
    c["ext"][:, :, 256:384] = c["ext_side"][...].astype(BF)

    def spread_channel(ch, _):
        wide = jnp.dot(c["ext"][ch], c["spread"][...], preferred_element_type=F32)
        for k in range(4):
            c["planar"][k, pl.ds(pl.multiple_of(ch * 96, 96), 96), :] = wide[:, 128 * k : 128 * k + 128]
        return 0

    lax.fori_loop(0, 9, spread_channel, 0, unroll=3)

    def gather_row(y, _):
        for k in range(4):
            c["rows_yc"][y, :, 128 * k : 128 * k + 128] = c["planar"][k, pl.ds(y + 12, 16, stride=96), :].astype(BF)
        return 0

    lax.fori_loop(0, 72, gather_row, 0, unroll=4)

    def column_caps(number, wp, origin, width):
        np_ = NP[number]
        n = 4 * np_
        cap = c["cap%d" % n]
        at = origin + 2 * iota((wp, n), 0) + (iota((wp, n), 1) // np_) % 2 + tx * width
        cap[0:wp, :] = jnp.where((at >= 0) & (at < width * cols_tx), BIG, 0.0)
        return cap

    def finish(number, r, cap, i0, g, wp, origin, height):
        np_ = NP[number]
        n = 4 * np_
        u = jnp.maximum(r + table[number : number + 1, 0:n], 0.0)
        pieces = []
        for k in range(g):
            at = origin + 2 * (i0 + k) + iota((1, n), 1) // (2 * np_) + ty * height
            row = jnp.where((at >= 0) & (at < height * rows_ty), BIG, 0.0)
            pieces.append(jnp.minimum(u[k * wp : (k + 1) * wp], jnp.minimum(cap[0:wp, :], row)))
        return pieces

    def to_blocks(pieces, target, i0, wp, n):
        t = c["t%d" % n]
        g = len(pieces)
        for k in range(g):
            t[k * wp : (k + 1) * wp, :] = pieces[k]
            target[i0 + k, :, 0:n] = pieces[k].astype(BF)
        for k in range(g):
            target[i0 + k, :, n : 2 * n] = t[k * wp + 1 : (k + 1) * wp + 1, :].astype(BF)

    def pooled(piece, np_):
        if np_ == 32:
            m = jnp.maximum(piece, pltpu.roll(piece, 64, 1))
            return jnp.maximum(m, pltpu.roll(m, 32, 1))
        if np_ == 64:
            m = jnp.maximum(piece[:, 0:128], piece[:, 128:256])
            return jnp.maximum(m, pltpu.roll(m, 64, 1))
        m = jnp.maximum(piece[:, 0:128], piece[:, 128:256])
        return jnp.maximum(m, jnp.maximum(piece[:, 256:384], piece[:, 384:512]))

    def pack(pixels, target, first, count, wp, lanes, row0, col0):
        lane = iota((wp, 128), 1)

        def step(i, _):
            a = [
                [pixels[row0 + 2 * i + py, pl.ds(col0 + m, wp, stride=2), :] for m in range(4)] for py in range(2)
            ]
            for u in range(2):
                four = [a[0][2 * u], a[0][2 * u + 1], a[1][2 * u], a[1][2 * u + 1]]
                base = u * 4 * lanes
                if lanes == 32:
                    v = jnp.where(
                        lane < 64,
                        jnp.where(lane < 32, four[0], four[1]),
                        jnp.where(lane < 96, four[2], four[3]),
                    )
                    target[i, :, base : base + 128] = v.astype(BF)
                elif lanes == 64:
                    for py in range(2):
                        v = jnp.where(lane < 64, four[2 * py], four[2 * py + 1])
                        target[i, :, base + 128 * py : base + 128 * py + 128] = v.astype(BF)
                else:
                    for q in range(4):
                        target[i, :, base + 128 * q : base + 128 * q + 128] = four[q].astype(BF)
            return 0

        lax.fori_loop(first, first + count, step, 0, unroll=True)

    def to_pixels(pieces, target, i0, wp, wr, np_):
        td = c["td"]
        lane = iota((wp, 128), 1)
        lane_r = iota((wr, 128), 1)
        for k in range(len(pieces)):
            for qy in range(2):
                at = 2 * k + qy
                if np_ == 128:
                    even = pieces[k][:, 256 * qy : 256 * qy + 128]
                    odd = pieces[k][:, 256 * qy + 128 : 256 * qy + 256]
                else:
                    v = pieces[k][:, 128 * qy : 128 * qy + 128]
                    w = pltpu.roll(v, 64, 1)
                    even = jnp.where(lane < 64, v, w)
                    odd = jnp.where(lane < 64, w, v)
                td[at, pl.ds(0, wp, stride=2), :] = even
                td[at, pl.ds(1, wp, stride=2), :] = odd
        for k in range(len(pieces)):
            for qy in range(2):
                at = 2 * k + qy
                here, right = td[at, 0:wr, :], td[at, 1 : wr + 1, :]
                if np_ == 128:
                    target[2 * (i0 + k) + qy, :, 0:128] = here.astype(BF)
                    target[2 * (i0 + k) + qy, :, 128:256] = right.astype(BF)
                else:
                    target[2 * (i0 + k) + qy, :, :] = jnp.where(lane_r < 64, here, right).astype(BF)

    def block_input(ref):
        def load(i0, g):
            lanes = ref.shape[2]
            rows = g * ref.shape[1]
            return [
                ref[pl.ds(i0, g)].reshape(rows, lanes),
                ref[pl.ds(i0 + 1, g)].reshape(rows, lanes),
            ]

        return load

    def layer(number, loads, first, count, g, wp, origin_y, origin_x, level, store):
        height, width = 32 >> level, 256 >> level
        cap = column_caps(number, wp, origin_x, width)

        def step(it, _):
            i0 = first + it * g
            lhs = []
            for load in loads:
                lhs = lhs + load(i0, g)
            lhs = jnp.concatenate(lhs, axis=1) if len(lhs) > 1 else lhs[0]
            if number in FLIPPED:
                r = jnp.dot(lhs, c["w%d" % number][...], preferred_element_type=F32)
            else:
                r = nt(lhs, c["w%d" % number][...])
            store(finish(number, r, cap, i0, g, wp, origin_y, height), i0)
            return 0

        if count == 1:
            step(0, 0)
        else:
            lax.fori_loop(0, count, step, 0)

    def pool_into(pixels, number, wp):
        def store(pieces, i0):
            for k, piece in enumerate(pieces):
                pixels[i0 + k, 0:wp, :] = pooled(piece, NP[number])

        return store

    def windows(first, count, g):
        t = c["t128"]

        def step(it, _):
            i0 = first + it * g
            for k in range(g):
                rows = c["rows_yc"][pl.ds(2 * (i0 + k), 4)].reshape(64, 512)
                stacked = jnp.concatenate([rows[:, 0:256], rows[:, 256:512]], axis=0)
                turned = nt(c["eye"][...], stacked)
                c["fwin"][i0 + k, :, 0:128] = turned.astype(BF)
                t[k * 160 : (k + 1) * 160, :] = turned
            for k in range(g):
                c["fwin"][i0 + k, :, 128:256] = t[k * 160 + 1 : (k + 1) * 160 + 1, :].astype(BF)
            return 0

        if count == 1:
            step(0, 0)
        else:
            lax.fori_loop(0, count, step, 0)

    def window_load(i0, g):
        return [c["fwin"][pl.ds(i0, g)].reshape(g * 160, 256)]

    def conv0(first, count, g):
        layer(0, [window_load], first, count, g, 160, -19, -35, 0, lambda p, i0: to_blocks(p, c["s1"], i0, 160, 128))

    def conv1(first, count, g):
        layer(1, [block_input(c["s1"])], first, count, g, 160, -18, -34, 0, pool_into(c["pix1"], 1, 160))

    def conv2(first, count, g):
        layer(2, [block_input(c["s2"])], first, count, g, 80, -8, -8, 1, pool_into(c["pix2"], 2, 80))

    windows(6, 2, 12)
    conv0(6, 2, 12)
    conv1(6, 2, 11)
    pack(c["pix1"], c["s2"], 3, 11, 80, 32, 0, 8)
    conv2(3, 1, 10)
    pack(c["pix2"], c["s3"], 0, 5, 48, 64, 3, 3)
    layer(3, [block_input(c["s3"])], 0, 1, 4, 48, 0, 0, 2, pool_into(c["pix3o"], 3, 48))

    lane16 = iota((16, 128), 1)
    for y in range(4):
        even = c["pix3o"][y, pl.ds(0, 16, stride=2), :]
        odd = c["pix3o"][y, pl.ds(1, 16, stride=2), :]
        c["tile_out"][16 * y : 16 * y + 16, :] = jnp.where(lane16 < 64, even, odd).astype(BF)
    copies = []
    for number, (dy, dx) in enumerate(FAR):
        copy = pltpu.make_async_remote_copy(
            src_ref=c["tile_out"],
            dst_ref=c["tiles_in"].at[number],
            send_sem=send2.at[number],
            recv_sem=recv2.at[number],
            device_id=device(dy, dx),
            device_id_type=MESH,
        )
        copy.start()
        copies.append(copy)

    windows(0, 1, 6)
    windows(30, 1, 5)
    conv0(0, 1, 6)
    conv0(30, 1, 5)
    conv1(0, 1, 6)
    conv1(28, 1, 6)
    pack(c["pix1"], c["s2"], 0, 3, 80, 32, 0, 8)
    pack(c["pix1"], c["s2"], 14, 3, 80, 32, 0, 8)
    conv2(0, 1, 3)
    conv2(13, 1, 3)
    pack(c["pix1"], c["k11"], 0, 12, 80, 32, 5, 13)
    pack(c["pix2"], c["k9"], 0, 8, 48, 64, 0, 0)

    for copy in copies:
        copy.wait()

    slot = {d: n for n, d in enumerate(FAR)}
    for ky in range(-3, 4):
        for kx in range(-1, 2):
            if (ky, kx) == (0, 0):
                tile = c["tile_out"][...].astype(F32)
            else:
                ok = (ty + ky >= 0) & (ty + ky < rows_ty) & (tx + kx >= 0) & (tx + kx < cols_tx)
                tile = jnp.where(jnp.where(ok, 1.0, 0.0) > 0, c["tiles_in"][slot[-ky, -kx]].astype(F32), 0.0)
            for y in range(4):
                if ky == -3 and y < 3 or ky == 3 and y > 0:
                    continue
                v = tile[16 * y : 16 * y + 16]
                w = pltpu.roll(v, 64, 1)
                row = 12 + 4 * ky + y
                col = 32 * (kx + 1)
                c["pix3"][row, pl.ds(col, 16, stride=2), :] = jnp.where(lane16 < 64, v, w)
                c["pix3"][row, pl.ds(col + 1, 16, stride=2), :] = jnp.where(lane16 < 64, w, v)

    pack(c["pix3"], c["s4"], 0, 11, 32, 64, 3, 23)
    pack(c["pix3"], c["k7"], 0, 6, 32, 64, 8, 28)

    layer(4, [block_input(c["s4"])], 0, 1, 10, 32, -8, -8, 3, pool_into(c["pix4"], 4, 32))
    pack(c["pix4"], c["s5"], 0, 5, 16, 128, 0, 0)
    layer(5, [block_input(c["s5"])], 0, 1, 4, 16, -3, -3, 4, lambda p, i0: to_blocks(p, c["s6"], i0, 16, 512))
    layer(6, [block_input(c["s6"])], 0, 1, 3, 16, -2, -2, 4, lambda p, i0: to_pixels(p, c["r7"], i0, 16, 32, 128))
    layer(
        7, [block_input(c["r7"]), block_input(c["k7"])], 0, 1, 5, 32, -3, -3, 3,
        lambda p, i0: to_blocks(p, c["s8"], i0, 32, 512),
    )
    layer(8, [block_input(c["s8"])], 0, 1, 4, 32, -2, -2, 3, lambda p, i0: to_pixels(p, c["r9"], i0, 32, 48, 128))
    layer(
        9, [block_input(c["r9"]), block_input(c["k9"])], 0, 1, 7, 48, -3, -3, 2,
        lambda p, i0: to_blocks(p, c["s10"], i0, 48, 512),
    )
    layer(10, [block_input(c["s10"])], 0, 1, 6, 48, -2, -2, 2, lambda p, i0: to_pixels(p, c["r11"], i0, 48, 80, 128))
    layer(
        11, [block_input(c["r11"]), block_input(c["k11"])], 0, 1, 11, 80, -3, -3, 1,
        lambda p, i0: to_blocks(p, c["s12"], i0, 80, 256),
    )
    layer(12, [block_input(c["s12"])], 0, 1, 10, 80, -2, -2, 1, lambda p, i0: to_pixels(p, c["r13"], i0, 80, 144, 64))

    def features_load(i0, g):
        return [c["fwin"][pl.ds(i0 + 8, g), 16:160, :].reshape(g * 144, 256)]

    layer(
        13, [block_input(c["r13"]), features_load], 0, 2, 10, 144, -3, -3, 0,
        lambda p, i0: to_blocks(p, c["s14"], i0, 144, 256),
    )
    layer(14, [block_input(c["s14"])], 0, 2, 9, 144, -2, -2, 0, lambda p, i0: to_blocks(p, c["s15"], i0, 144, 128))

    lane144 = iota((16, 144), 1)

    def last(i, _):
        field = jnp.concatenate([c["s15"][i], c["s15"][i + 1]], axis=1)
        r = nt(c["w15"][...], field) + c["column"][...]
        r = jnp.where(lane144 < 129, r, 0.0)
        c["z0"][pl.ds(pl.multiple_of(8 * i, 8), 8), :] = r[0:8]
        c["z1"][pl.ds(pl.multiple_of(8 * i, 8), 8), :] = r[8:16]
        return 0

    c["z0"][136:144, :] = jnp.zeros((8, 144), F32)
    c["z1"][136:144, :] = jnp.zeros((8, 144), F32)
    lax.fori_loop(0, 17, last, 0, unroll=17)
    at = iota((144, 256), 1) - 2 * iota((144, 256), 0)
    even = (at == -1).astype(F32).astype(BF)
    odd = (at == 0).astype(F32).astype(BF)
    wide = jnp.dot(c["z0"][...].astype(BF), even, preferred_element_type=F32) + jnp.dot(
        c["z1"][...].astype(BF), odd, preferred_element_type=F32
    )
    for half in range(2):
        lanes = slice(128 * half, 128 * half + 128)
        c["zf"][half] = wide[:, lanes]
        for o in range(3):
            c["out32"][2 * o + half, pl.ds(0, 16, stride=2), :] = c["zf"][half, pl.ds(3 + o, 16, stride=8), :]
            c["out32"][2 * o + half, pl.ds(1, 16, stride=2), :] = c["zf"][half, pl.ds(8 + o, 16, stride=8), :]
            out[o, :, lanes] = c["out32"][2 * o + half].astype(BF)


def body(sizes, features, *rest):
    weights, biases = list(rest[:16]), rest[16]
    for number in FLIPPED:
        weights[number] = jnp.transpose(weights[number], (0, 1, 3, 2) if number else (0, 3, 1, 2))
    vmem = pl.BlockSpec(memory_space=pltpu.VMEM)
    scratch = [pltpu.VMEM(shape, kind) for shape, kind in SCRATCH.values()]
    scratch += [pltpu.SemaphoreType.DMA((n,)) for n in (8, 8, 20, 20)]
    return pl.pallas_call(
        functools.partial(kernel, sizes),
        out_shape=jax.ShapeDtypeStruct((3, 32, 256), BF),
        in_specs=[vmem] * 18,
        out_specs=vmem,
        scratch_shapes=scratch,
        compiler_params=pltpu.CompilerParams(
            collective_id=0, has_side_effects=True, vmem_limit_bytes=58 << 20
        ),
    )(features, *weights, biases)


def solution(mesh):
    sizes = (mesh.shape["ty"], mesh.shape["tx"])
    return jax.shard_map(
        functools.partial(body, sizes),
        mesh=mesh,
        in_specs=(P(None, "ty", "tx"),) + (P(),) * 17,
        out_specs=P(None, "ty", "tx"),
        check_vma=False,
    )
```

```python
import functools

import jax
import jax.numpy as jnp
from jax import lax
from jax.experimental import pallas as pl
from jax.experimental.pallas import tpu as pltpu
from jax.sharding import PartitionSpec as P

F32 = jnp.float32
BF = jnp.bfloat16
BIG = 3.0e38
MESH = pl.DeviceIdType.MESH

COUT = [32, 32, 48, 64, 80, 96, 96, 112, 112, 96, 96, 64, 64, 64, 32, 3]
CIN = [9, 32, 32, 48, 64, 80, 96, 160, 112, 160, 96, 128, 64, 73, 64, 32]
NP = [32, 32, 64, 64, 128, 128, 128, 128, 128, 128, 128, 64, 64, 64, 32, 4]
KDIM = [256, 256, 512, 1024, 1024, 2048, 2048, 1536, 2048, 1536, 2048, 1024, 1024, 512, 512, 256]
SPLIT = (1, 14, 15)
DIRS = [(dy, dx) for dy in (-1, 0, 1) for dx in (-1, 0, 1) if (dy, dx) != (0, 0)]
FAR = DIRS + [(dy, dx) for dy in (-3, -2, 2, 3) for dx in (-1, 0, 1)]

SCRATCH = dict(
    rows_in=((2, 9, 32, 256), BF),
    cols_out=((2, 80, 128), BF),
    cols_in=((6, 80, 128), BF),
    tile_out=((64, 128), BF),
    tiles_in=((20, 64, 128), BF),
    ext_side=((9, 96, 128), F32),
    ext=((9, 96, 384), BF),
    spread=((384, 512), BF),
    planar=((4, 16 * 96, 128), F32),
    rows_yc=((72, 16, 512), BF),
    eye=((160, 256), BF),
    fwin=((40, 160, 256), BF),
    s1=((36, 160, 128), BF),
    pix1=((34, 176, 128), F32),
    s2=((17, 80, 256), BF),
    pix2=((16, 112, 128), F32),
    s3=((5, 48, 512), BF),
    pix3o=((4, 48, 128), F32),
    pix3=((28, 112, 128), F32),
    s4=((11, 32, 512), BF),
    pix4=((10, 48, 128), F32),
    s5=((5, 16, 1024), BF),
    s6=((4, 16, 1024), BF),
    r7=((6, 32, 256), BF),
    k7=((6, 32, 512), BF),
    s8=((5, 32, 1024), BF),
    r9=((8, 48, 256), BF),
    k9=((8, 48, 512), BF),
    s10=((7, 48, 1024), BF),
    r11=((12, 80, 256), BF),
    k11=((12, 80, 256), BF),
    s12=((11, 80, 512), BF),
    r13=((24, 144, 128), BF),
    s14=((21, 144, 256), BF),
    s15=((20, 144, 128), BF),
    t128=((1928, 128), F32),
    t256=((1448, 256), F32),
    t512=((360, 512), F32),
    td=((20, 184, 128), F32),
    cap128=((160, 128), F32),
    cap256=((144, 256), F32),
    cap512=((48, 512), F32),
    w15f=((32, 256), F32),
    flat=((16, 128), F32),
    table=((16, 512), F32),
    column=((16, 144), F32),
    z0=((144, 144), F32),
    z1=((144, 144), F32),
    zf=((2, 144, 128), F32),
    out32=((6, 32, 128), F32),
)
for _k in range(16):
    _n = 32 if _k == 15 else 256 if _k in SPLIT else 4 * NP[_k]
    SCRATCH["w%d" % _k] = ((KDIM[_k], _n) if _k in (0, 2, 3, 4, 5, 7, 9) else (_n, KDIM[_k]), BF)


def iota(shape, dim):
    return lax.broadcasted_iota(jnp.int32, shape, dim)


def nt(a, b):
    return lax.dot_general(a, b, (((1,), (1,)), ((), ())), preferred_element_type=F32)


FLIPPED = (0, 2, 3, 4, 5, 7, 9)


def tap_of(w, number, ky, kx, first, count):
    if number == 0:
        return w[ky, :, kx, :]
    if number in FLIPPED:
        return w[ky, kx, first : first + count, :]
    return w[ky, kx][:, first : first + count]


def put(wt, number, n, k, tap):
    if number in FLIPPED:
        wt[k : k + tap.shape[0], n : n + tap.shape[1]] = tap
    else:
        wt[n : n + tap.shape[0], k : k + tap.shape[1]] = tap


def prepare_blocks(wt, w, number, offset, first, count, lanes):
    for ky in range(3):
        for kx in range(3):
            tap = tap_of(w, number, ky, kx, first, count)
            for qy in range(2):
                for qx in range(2):
                    r, s = ky + qy, kx + qx
                    n = (qy * 2 + qx) * NP[number]
                    if number in SPLIT:
                        k = (r // 2 * 4 + r % 2 * 2 + s % 2) * lanes
                        n = n + s // 2 * 128
                    else:
                        k = offset + ((r // 2 * 2 + s // 2) * 4 + r % 2 * 2 + s % 2) * lanes
                    put(wt, number, n, k, tap)


def prepare_window(wt, w, number, offset, first):
    for ky in range(3):
        for kx in range(3):
            tap = tap_of(w, number, ky, kx, first, 9)
            for qy in range(2):
                for qx in range(2):
                    k = offset + (kx + qx) * 64 + (ky + qy) * 16
                    put(wt, number, (qy * 2 + qx) * NP[number], k, tap)


SUMS = {(0, 0): (0, 1), (0, 1): (2,), (1, 0): (0,), (1, 1): (1, 2)}


def prepare_up(wt, w, number, count, lanes):
    taps = [[tap_of(w, number, ky, kx, 0, count).astype(F32) for kx in range(3)] for ky in range(3)]
    for qy in range(2):
        for t in range(2):
            rows = SUMS[qy, t]
            line = taps[rows[0]] if len(rows) == 1 else [taps[rows[0]][kx] + taps[rows[1]][kx] for kx in range(3)]
            for qx in range(2):
                for u in range(2):
                    cols = SUMS[qx, u]
                    total = line[cols[0]] if len(cols) == 1 else line[cols[0]] + line[cols[1]]
                    put(wt, number, (qy * 2 + qx) * NP[number], (t * 2 + u) * lanes, total.astype(BF))


def prepare_biases(biases, flat, table, column):
    flat[...] = jnp.zeros(flat.shape, F32)
    for r in range(8):
        flat[r : r + 1, :] = biases[pl.ds(128 * r, 128)].reshape(1, 128)
    flat[8:9, 0:67] = biases[pl.ds(1024, 67)].reshape(1, 67)
    lane = iota((8, 128), 1)
    offset = 0
    for number in range(16):
        r, m = offset // 128, offset % 128
        offset = offset + COUT[number]
        pair = jnp.concatenate([flat[r : r + 1, :], flat[r + 1 : r + 2, :]], axis=1)
        pair = jnp.broadcast_to(pair, (8, 256))
        if m:
            pair = pltpu.roll(pair, 256 - m, 1)
        value = jnp.where(lane < COUT[number], pair[:, 0:128], 0.0)
        if number == 15:
            row = iota((16, 128), 0) % 8
            twice = jnp.concatenate([value, value], axis=0)
            mine = jnp.where((iota((16, 128), 1) == row % 3) & (row < 6), twice, 0.0)
            column[...] = jnp.broadcast_to(jnp.sum(mine, axis=1, keepdims=True), (16, 144))
            continue
        if NP[number] == 32:
            value = value + pltpu.roll(value, 32, 1)
        if NP[number] <= 64:
            value = value + pltpu.roll(value, 64, 1)
        for k in range(4 * NP[number] // 128):
            table[number : number + 1, 128 * k : 128 * k + 128] = value[0:1]


def kernel(sizes, feat, *refs):
    rows_ty, cols_tx = sizes
    sources = refs[:16]
    weights = refs[-17:-1]
    weight_sem = refs[-1]
    loads = [pltpu.make_async_copy(sources[k], weights[k], weight_sem.at[k]) for k in range(16)]
    for load in loads:
        load.start()
    out = refs[17]
    c = dict(zip(SCRATCH, refs[18 : 18 + len(SCRATCH)]))
    send1, recv1, send2, recv2 = refs[18 + len(SCRATCH) : 22 + len(SCRATCH)]
    table = c["table"]
    ty = lax.axis_index("ty")
    tx = lax.axis_index("tx")

    def device(dy, dx):
        return (lax.rem(ty + dy + rows_ty, rows_ty), lax.rem(tx + dx + cols_tx, cols_tx))

    barrier = pltpu.get_barrier_semaphore()
    for dy, dx in FAR:
        pl.semaphore_signal(barrier, inc=1, device_id=device(dy, dx), device_id_type=MESH)

    lane9 = iota((9, 8, 128), 2)
    for side in range(2):
        value = jnp.zeros((9, 8, 128), F32)
        for g in range(4):
            piece = feat[:, 8 * g : 8 * g + 8, 128 * side : 128 * side + 128].astype(F32)
            shift = (32 * g - 96 * side) % 128
            if shift:
                piece = pltpu.roll(piece, shift, 2)
            value = jnp.where((lane9 >= 32 * g) & (lane9 < 32 * g + 32), piece, value)
        c["cols_out"][side, 0:72, :] = value.reshape(72, 128).astype(BF)
        c["cols_out"][side, 64:80, :] = jnp.concatenate(
            [value.reshape(72, 128)[64:72], jnp.zeros((8, 128), F32)], 0
        ).astype(BF)

    def clear(number):
        c["w%d" % number][...] = jnp.zeros(c["w%d" % number].shape, BF)

    for number in range(4):
        clear(number)
    for load in loads[:4]:
        load.wait()
    prepare_window(c["w0"], weights[0], 0, 0, 0)
    prepare_blocks(c["w1"], weights[1], 1, 0, 0, 32, 32)
    prepare_blocks(c["w2"], weights[2], 2, 0, 0, 32, 32)
    prepare_blocks(c["w3"], weights[3], 3, 0, 0, 48, 64)
    prepare_biases(refs[16], c["flat"], c["table"], c["column"])

    place = iota((384, 128), 0)
    x = jnp.where(place < 256, place, jnp.where(place < 288, place - 288, jnp.where(place < 320, place - 32, -1000)))
    x = x - 2 * iota((384, 128), 1) + 36
    for px in range(2):
        for half in range(2):
            hit = jnp.where(x == px + 256 * half, 1.0, 0.0)
            c["spread"][:, 256 * px + 128 * half : 256 * px + 128 * half + 128] = hit.astype(BF)
    c["eye"][...] = (iota((160, 256), 0) == iota((160, 256), 1)).astype(F32).astype(BF)
    for k in range(4):
        c["planar"][k, 864:1536, :] = jnp.zeros((672, 128), F32)

    pl.semaphore_wait(barrier, len(FAR))
    copies = []
    for number, (dy, dx) in enumerate(DIRS):
        if dx == 0:
            source, target = feat, c["rows_in"].at[0 if dy == 1 else 1]
        else:
            source = c["cols_out"].at[0 if dx == -1 else 1]
            target = c["cols_in"].at[(0 if dx == -1 else 3) + dy + 1]
        copy = pltpu.make_async_remote_copy(
            src_ref=source,
            dst_ref=target,
            send_sem=send1.at[number],
            recv_sem=recv1.at[number],
            device_id=device(dy, dx),
            device_id_type=MESH,
        )
        copy.start()
        copies.append(copy)

    for number in range(4, 15):
        clear(number)
    for load in loads[4:]:
        load.wait()
    prepare_blocks(c["w4"], weights[4], 4, 0, 0, 64, 64)
    prepare_blocks(c["w5"], weights[5], 5, 0, 0, 80, 128)
    prepare_blocks(c["w6"], weights[6], 6, 0, 0, 96, 128)
    prepare_up(c["w7"], weights[7], 7, 96, 128)
    prepare_blocks(c["w7"], weights[7], 7, 512, 96, 64, 64)
    prepare_blocks(c["w8"], weights[8], 8, 0, 0, 112, 128)
    prepare_up(c["w9"], weights[9], 9, 112, 128)
    prepare_blocks(c["w9"], weights[9], 9, 512, 112, 48, 64)
    prepare_blocks(c["w10"], weights[10], 10, 0, 0, 96, 128)
    prepare_up(c["w11"], weights[11], 11, 96, 128)
    prepare_blocks(c["w11"], weights[11], 11, 512, 96, 32, 32)
    prepare_blocks(c["w12"], weights[12], 12, 0, 0, 64, 64)
    prepare_up(c["w13"], weights[13], 13, 64, 64)
    prepare_window(c["w13"], weights[13], 13, 256, 64)
    prepare_blocks(c["w14"], weights[14], 14, 0, 0, 64, 64)
    c["w15f"][...] = jnp.zeros((32, 256), F32)
    for ky in range(3):
        for kx in range(3):
            tap = weights[15][ky, kx].astype(F32)
            for qy in range(2):
                for qx in range(2):
                    r, s = ky + qy, kx + qx
                    k = (r // 2 * 4 + r % 2 * 2 + s % 2) * 32
                    n = s // 2 * 16 + qx * 8 + qy * 3
                    c["w15f"][n : n + 3, k : k + 32] = tap
    c["w15"][...] = c["w15f"][...].astype(BF)
    for copy in copies:
        copy.wait()

    first_row = jnp.where(ty > 0, 1.0, 0.0)
    last_row = jnp.where(ty < rows_ty - 1, 1.0, 0.0)
    first_col = jnp.where(tx > 0, 1.0, 0.0)
    last_col = jnp.where(tx < cols_tx - 1, 1.0, 0.0)
    c["ext"][:, 0:32, 0:256] = jnp.where(first_row > 0, c["rows_in"][0].astype(F32), 0.0).astype(BF)
    c["ext"][:, 32:64, 0:256] = feat[...]
    c["ext"][:, 64:96, 0:256] = jnp.where(last_row > 0, c["rows_in"][1].astype(F32), 0.0).astype(BF)
    for k in range(3):
        row_ok = (first_row, 1.0, last_row)[k]
        left = c["cols_in"][3 + (1, 0, -1)[k] + 1].astype(F32)[0:72].reshape(9, 8, 128)
        right = c["cols_in"][(1, 0, -1)[k] + 1].astype(F32)[0:72].reshape(9, 8, 128)
        left = jnp.where(row_ok * first_col > 0, left, 0.0)
        right = jnp.where(row_ok * last_col > 0, right, 0.0)
        for g in range(4):
            to_left = pltpu.roll(left, (128 - 32 * g) % 128, 2) if g else left
            to_right = pltpu.roll(right, (160 - 32 * g) % 128, 2) if g != 1 else right
            piece = jnp.where(lane9 < 32, to_left, jnp.where(lane9 < 64, to_right, 0.0))
            c["ext_side"][:, 32 * k + 8 * g : 32 * k + 8 * g + 8, :] = piece
    c["ext"][:, :, 256:384] = c["ext_side"][...].astype(BF)

    def spread_channel(ch, _):
        wide = jnp.dot(c["ext"][ch], c["spread"][...], preferred_element_type=F32)
        for k in range(4):
            c["planar"][k, pl.ds(pl.multiple_of(ch * 96, 96), 96), :] = wide[:, 128 * k : 128 * k + 128]
        return 0

    lax.fori_loop(0, 9, spread_channel, 0, unroll=3)

    def gather_row(y, _):
        for k in range(4):
            c["rows_yc"][y, :, 128 * k : 128 * k + 128] = c["planar"][k, pl.ds(y + 12, 16, stride=96), :].astype(BF)
        return 0

    lax.fori_loop(0, 72, gather_row, 0, unroll=4)

    def column_caps(number, wp, origin, width):
        np_ = NP[number]
        n = 4 * np_
        cap = c["cap%d" % n]
        at = origin + 2 * iota((wp, n), 0) + (iota((wp, n), 1) // np_) % 2 + tx * width
        cap[0:wp, :] = jnp.where((at >= 0) & (at < width * cols_tx), BIG, 0.0)
        return cap

    def finish(number, r, cap, i0, g, wp, origin_y, origin_x, height, width):
        np_ = NP[number]
        n = 4 * np_
        u = jnp.maximum(r + table[number : number + 1, 0:n], 0.0)
        low = -(origin_x // 2) if origin_x < 0 else 0
        high = (width - origin_x) // 2
        low, high = (low + 7) // 8 * 8, min(high // 8 * 8, wp)
        pieces = []
        for k in range(g):
            v = u[k * wp : (k + 1) * wp]
            parts = [jnp.minimum(v[0:low], cap[0:low, :]), v[low:high], jnp.minimum(v[high:wp], cap[high:wp, :])]
            v = jnp.concatenate([p for p in parts if p.shape[0]], axis=0)
            y = origin_y + 2 * (i0 + k)
            if y < 0 or y + 2 > height:
                at = y + iota((1, n), 1) // (2 * np_) + ty * height
                v = jnp.minimum(v, jnp.where((at >= 0) & (at < height * rows_ty), BIG, 0.0))
            pieces.append(v)
        return pieces

    def to_blocks(pieces, target, i0, wp, n):
        t = c["t%d" % n]
        g = len(pieces)
        if target.shape[2] == n:
            for k in range(g):
                target[i0 + k, :, :] = pieces[k].astype(BF)
            return
        for k in range(g):
            t[k * wp : (k + 1) * wp, :] = pieces[k]
            target[i0 + k, :, 0:n] = pieces[k].astype(BF)
        for k in range(g):
            target[i0 + k, :, n : 2 * n] = t[k * wp + 1 : (k + 1) * wp + 1, :].astype(BF)

    def pooled(piece, np_):
        if np_ == 32:
            m = jnp.maximum(piece, pltpu.roll(piece, 64, 1))
            return jnp.maximum(m, pltpu.roll(m, 32, 1))
        if np_ == 64:
            m = jnp.maximum(piece[:, 0:128], piece[:, 128:256])
            return jnp.maximum(m, pltpu.roll(m, 64, 1))
        m = jnp.maximum(piece[:, 0:128], piece[:, 128:256])
        return jnp.maximum(m, jnp.maximum(piece[:, 256:384], piece[:, 384:512]))

    def pack(pixels, target, first, count, wp, lanes, row0, col0):
        lane = iota((wp, 128), 1)

        def step(i, _):
            a = [
                [pixels[row0 + 2 * i + py, pl.ds(col0 + m, wp, stride=2), :] for m in range(4)] for py in range(2)
            ]
            for u in range(2):
                four = [a[0][2 * u], a[0][2 * u + 1], a[1][2 * u], a[1][2 * u + 1]]
                base = u * 4 * lanes
                if lanes == 32:
                    v = jnp.where(
                        lane < 64,
                        jnp.where(lane < 32, four[0], four[1]),
                        jnp.where(lane < 96, four[2], four[3]),
                    )
                    target[i, :, base : base + 128] = v.astype(BF)
                elif lanes == 64:
                    for py in range(2):
                        v = jnp.where(lane < 64, four[2 * py], four[2 * py + 1])
                        target[i, :, base + 128 * py : base + 128 * py + 128] = v.astype(BF)
                else:
                    for q in range(4):
                        target[i, :, base + 128 * q : base + 128 * q + 128] = four[q].astype(BF)
            return 0

        lax.fori_loop(first, first + count, step, 0, unroll=True)

    def to_pixels(pieces, target, i0, wp, wr, np_):
        td = c["td"]
        lane = iota((wp, 128), 1)
        lane_r = iota((wr, 128), 1)
        for k in range(len(pieces)):
            for qy in range(2):
                at = 2 * k + qy
                if np_ == 128:
                    even = pieces[k][:, 256 * qy : 256 * qy + 128]
                    odd = pieces[k][:, 256 * qy + 128 : 256 * qy + 256]
                else:
                    v = pieces[k][:, 128 * qy : 128 * qy + 128]
                    w = pltpu.roll(v, 64, 1)
                    even = jnp.where(lane < 64, v, w)
                    odd = jnp.where(lane < 64, w, v)
                td[at, pl.ds(0, wp, stride=2), :] = even
                td[at, pl.ds(1, wp, stride=2), :] = odd
        for k in range(len(pieces)):
            for qy in range(2):
                at = 2 * k + qy
                here, right = td[at, 0:wr, :], td[at, 1 : wr + 1, :]
                if np_ == 128:
                    target[2 * (i0 + k) + qy, :, 0:128] = here.astype(BF)
                    target[2 * (i0 + k) + qy, :, 128:256] = right.astype(BF)
                else:
                    target[2 * (i0 + k) + qy, :, :] = jnp.where(lane_r < 64, here, right).astype(BF)

    def block_input(ref):
        def load(i0, g):
            lanes = ref.shape[2]
            rows = g * ref.shape[1]
            return [
                ref[pl.ds(i0, g)].reshape(rows, lanes),
                ref[pl.ds(i0 + 1, g)].reshape(rows, lanes),
            ]

        return load

    def layer(number, loads, first, count, g, wp, origin_y, origin_x, level, store):
        height, width = 32 >> level, 256 >> level
        cap = column_caps(number, wp, origin_x, width)

        def step(it, _):
            i0 = first + it * g
            lhs = []
            for load in loads:
                lhs = lhs + load(i0, g)
            lhs = jnp.concatenate(lhs, axis=1) if len(lhs) > 1 else lhs[0]
            if number in FLIPPED:
                r = jnp.dot(lhs, c["w%d" % number][...], preferred_element_type=F32)
            else:
                r = nt(lhs, c["w%d" % number][...])
            if number in SPLIT:
                c["t128"][0 : g * wp, :] = r[:, 128:256]
                r = r[:, 0:128] + c["t128"][1 : g * wp + 1, :]
            store(finish(number, r, cap, i0, g, wp, origin_y, origin_x, height, width), i0)
            return 0

        for it in range(count):
            step(it, 0)

    def pool_into(pixels, number, wp):
        def store(pieces, i0):
            for k, piece in enumerate(pieces):
                pixels[i0 + k, 0:wp, :] = pooled(piece, NP[number])

        return store

    def windows(first, count, g):
        t = c["t128"]

        def step(it, _):
            i0 = first + it * g
            for k in range(g):
                rows = c["rows_yc"][pl.ds(2 * (i0 + k), 4)].reshape(64, 512)
                stacked = jnp.concatenate([rows[:, 0:256], rows[:, 256:512]], axis=0)
                turned = nt(c["eye"][...], stacked)
                c["fwin"][i0 + k, :, 0:128] = turned.astype(BF)
                t[k * 160 : (k + 1) * 160, :] = turned
            for k in range(g):
                c["fwin"][i0 + k, :, 128:256] = t[k * 160 + 1 : (k + 1) * 160 + 1, :].astype(BF)
            return 0

        if count == 1:
            step(0, 0)
        else:
            lax.fori_loop(0, count, step, 0)

    def window_load(i0, g):
        return [c["fwin"][pl.ds(i0, g)].reshape(g * 160, 256)]

    def conv0(first, count, g):
        layer(0, [window_load], first, count, g, 160, -19, -35, 0, lambda p, i0: to_blocks(p, c["s1"], i0, 160, 128))

    def conv1(first, count, g):
        layer(1, [block_input(c["s1"])], first, count, g, 160, -18, -34, 0, pool_into(c["pix1"], 1, 160))

    def conv2(first, count, g):
        layer(2, [block_input(c["s2"])], first, count, g, 80, -8, -8, 1, pool_into(c["pix2"], 2, 80))

    windows(6, 2, 12)
    conv0(6, 2, 12)
    conv1(6, 2, 11)
    pack(c["pix1"], c["s2"], 3, 11, 80, 32, 0, 8)
    conv2(3, 1, 10)
    pack(c["pix2"], c["s3"], 0, 5, 48, 64, 3, 3)
    layer(3, [block_input(c["s3"])], 0, 1, 4, 48, 0, 0, 2, pool_into(c["pix3o"], 3, 48))

    lane8 = iota((8, 128), 1)
    pieces = []
    for half in range(2):
        for y in range(4):
            even = c["pix3o"][y, pl.ds(16 * half, 8, stride=2), :]
            odd = c["pix3o"][y, pl.ds(16 * half + 1, 8, stride=2), :]
            pieces.append(jnp.where(lane8 < 64, even, odd))
    c["tile_out"][...] = jnp.concatenate(pieces, axis=0).astype(BF)
    copies = []
    for number, (dy, dx) in enumerate(FAR):
        rows = pl.ds(0, 64) if dx == 0 else pl.ds(32, 32) if dx == 1 else pl.ds(0, 32)
        copy = pltpu.make_async_remote_copy(
            src_ref=c["tile_out"].at[rows],
            dst_ref=c["tiles_in"].at[number, rows],
            send_sem=send2.at[number],
            recv_sem=recv2.at[number],
            device_id=device(dy, dx),
            device_id_type=MESH,
        )
        copy.start()
        copies.append(copy)

    windows(0, 1, 6)
    windows(30, 1, 5)
    conv0(0, 1, 6)
    conv0(30, 1, 5)
    conv1(0, 1, 6)
    conv1(28, 1, 6)
    pack(c["pix1"], c["s2"], 0, 3, 80, 32, 0, 8)
    pack(c["pix1"], c["s2"], 14, 3, 80, 32, 0, 8)
    conv2(0, 1, 3)
    conv2(13, 1, 3)
    pack(c["pix1"], c["k11"], 0, 12, 80, 32, 5, 13)
    pack(c["pix2"], c["k9"], 0, 8, 48, 64, 0, 0)

    for copy in copies:
        copy.wait()

    slot = {d: n for n, d in enumerate(FAR)}
    for ky in range(-3, 4):
        for kx in range(-1, 2):
            if (ky, kx) == (0, 0):
                tile = c["tile_out"][...].astype(F32)
            else:
                ok = (ty + ky >= 0) & (ty + ky < rows_ty) & (tx + kx >= 0) & (tx + kx < cols_tx)
                tile = jnp.where(jnp.where(ok, 1.0, 0.0) > 0, c["tiles_in"][slot[-ky, -kx]].astype(F32), 0.0)
            halves = (0, 1) if kx == 0 else (1,) if kx == -1 else (0,)
            for y in range(4):
                if ky == -3 and y < 3 or ky == 3 and y > 0:
                    continue
                for half in halves:
                    v = tile[32 * half + 8 * y : 32 * half + 8 * y + 8]
                    w = pltpu.roll(v, 64, 1)
                    row = 12 + 4 * ky + y
                    col = 32 * (kx + 1) + 16 * half
                    c["pix3"][row, pl.ds(col, 8, stride=2), :] = jnp.where(lane8 < 64, v, w)
                    c["pix3"][row, pl.ds(col + 1, 8, stride=2), :] = jnp.where(lane8 < 64, w, v)

    pack(c["pix3"], c["s4"], 0, 11, 32, 64, 3, 23)
    pack(c["pix3"], c["k7"], 0, 6, 32, 64, 8, 28)

    layer(4, [block_input(c["s4"])], 0, 1, 10, 32, -8, -8, 3, pool_into(c["pix4"], 4, 32))
    pack(c["pix4"], c["s5"], 0, 5, 16, 128, 0, 0)
    layer(5, [block_input(c["s5"])], 0, 1, 4, 16, -3, -3, 4, lambda p, i0: to_blocks(p, c["s6"], i0, 16, 512))
    layer(6, [block_input(c["s6"])], 0, 1, 3, 16, -2, -2, 4, lambda p, i0: to_pixels(p, c["r7"], i0, 16, 32, 128))
    layer(
        7, [block_input(c["r7"]), block_input(c["k7"])], 0, 1, 5, 32, -3, -3, 3,
        lambda p, i0: to_blocks(p, c["s8"], i0, 32, 512),
    )
    layer(8, [block_input(c["s8"])], 0, 1, 4, 32, -2, -2, 3, lambda p, i0: to_pixels(p, c["r9"], i0, 32, 48, 128))
    layer(
        9, [block_input(c["r9"]), block_input(c["k9"])], 0, 1, 7, 48, -3, -3, 2,
        lambda p, i0: to_blocks(p, c["s10"], i0, 48, 512),
    )
    layer(10, [block_input(c["s10"])], 0, 1, 6, 48, -2, -2, 2, lambda p, i0: to_pixels(p, c["r11"], i0, 48, 80, 128))
    layer(
        11, [block_input(c["r11"]), block_input(c["k11"])], 0, 1, 11, 80, -3, -3, 1,
        lambda p, i0: to_blocks(p, c["s12"], i0, 80, 256),
    )
    layer(12, [block_input(c["s12"])], 0, 1, 10, 80, -2, -2, 1, lambda p, i0: to_pixels(p, c["r13"], i0, 80, 144, 64))

    def features_load(i0, g):
        return [c["fwin"][pl.ds(i0 + 8, g), 16:160, :].reshape(g * 144, 256)]

    layer(
        13, [block_input(c["r13"]), features_load], 0, 1, 10, 144, -3, -3, 0,
        lambda p, i0: to_blocks(p, c["s14"], i0, 144, 256),
    )
    layer(
        13, [block_input(c["r13"]), features_load], 10, 1, 9, 144, -3, -3, 0,
        lambda p, i0: to_blocks(p, c["s14"], i0, 144, 256),
    )
    layer(14, [block_input(c["s14"])], 0, 2, 9, 144, -2, -2, 0, lambda p, i0: to_blocks(p, c["s15"], i0, 144, 128))

    lane144 = iota((16, 144), 1)

    def last(i, _):
        field = jnp.concatenate([c["s15"][i], c["s15"][i + 1]], axis=1)
        r = nt(c["w15"][...], field)
        r = r[0:16] + pltpu.roll(r[16:32], 143, 1) + c["column"][...]
        r = jnp.where(lane144 < 129, r, 0.0)
        c["z0"][pl.ds(pl.multiple_of(8 * i, 8), 8), :] = r[0:8]
        c["z1"][pl.ds(pl.multiple_of(8 * i, 8), 8), :] = r[8:16]
        return 0

    c["z0"][136:144, :] = jnp.zeros((8, 144), F32)
    c["z1"][136:144, :] = jnp.zeros((8, 144), F32)
    lax.fori_loop(0, 17, last, 0, unroll=17)
    at = iota((144, 256), 1) - 2 * iota((144, 256), 0)
    even = (at == -1).astype(F32).astype(BF)
    odd = (at == 0).astype(F32).astype(BF)
    wide = jnp.dot(c["z0"][...].astype(BF), even, preferred_element_type=F32) + jnp.dot(
        c["z1"][...].astype(BF), odd, preferred_element_type=F32
    )
    for half in range(2):
        lanes = slice(128 * half, 128 * half + 128)
        c["zf"][half] = wide[:, lanes]
        for o in range(3):
            c["out32"][2 * o + half, pl.ds(0, 16, stride=2), :] = c["zf"][half, pl.ds(3 + o, 16, stride=8), :]
            c["out32"][2 * o + half, pl.ds(1, 16, stride=2), :] = c["zf"][half, pl.ds(8 + o, 16, stride=8), :]
            out[o, :, lanes] = c["out32"][2 * o + half].astype(BF)


def body(sizes, features, *rest):
    weights, biases = list(rest[:16]), rest[16]
    for number in FLIPPED:
        weights[number] = jnp.transpose(weights[number], (0, 1, 3, 2) if number else (0, 3, 1, 2))
    vmem = pl.BlockSpec(memory_space=pltpu.VMEM)
    scratch = [pltpu.VMEM(shape, kind) for shape, kind in SCRATCH.values()]
    scratch += [pltpu.SemaphoreType.DMA((n,)) for n in (8, 8, 20, 20)]
    scratch += [pltpu.VMEM(w.shape, BF) for w in weights] + [pltpu.SemaphoreType.DMA((16,))]
    return pl.pallas_call(
        functools.partial(kernel, sizes),
        out_shape=jax.ShapeDtypeStruct((3, 32, 256), BF),
        in_specs=[vmem] + [pl.BlockSpec(memory_space=pl.ANY)] * 16 + [vmem],
        out_specs=vmem,
        scratch_shapes=scratch,
        compiler_params=pltpu.CompilerParams(
            collective_id=0, has_side_effects=True, vmem_limit_bytes=58 << 20
        ),
    )(features, *weights, biases)


def solution(mesh):
    sizes = (mesh.shape["ty"], mesh.shape["tx"])
    return jax.shard_map(
        functools.partial(body, sizes),
        mesh=mesh,
        in_specs=(P(None, "ty", "tx"),) + (P(),) * 17,
        out_specs=P(None, "ty", "tx"),
        check_vma=False,
    )
```

```python
import functools

import jax
import jax.numpy as jnp
from jax import lax
from jax.experimental import pallas as pl
from jax.experimental.pallas import tpu as pltpu
from jax.sharding import PartitionSpec as P

F32 = jnp.float32
BF = jnp.bfloat16
BIG = 3.0e38
MESH = pl.DeviceIdType.MESH

COUT = [32, 32, 48, 64, 80, 96, 96, 112, 112, 96, 96, 64, 64, 64, 32, 3]
CIN = [9, 32, 32, 48, 64, 80, 96, 160, 112, 160, 96, 128, 64, 73, 64, 32]
NP = [32, 32, 64, 64, 128, 128, 128, 128, 128, 128, 128, 64, 64, 64, 32, 4]
KDIM = [256, 256, 512, 1024, 1024, 2048, 2048, 1536, 2048, 1536, 2048, 1024, 1024, 512, 512, 256]
SPLIT = (1, 14, 15)
DIRS = [(dy, dx) for dy in (-1, 0, 1) for dx in (-1, 0, 1) if (dy, dx) != (0, 0)]
FAR = DIRS + [(dy, dx) for dy in (-3, -2, 2, 3) for dx in (-1, 0, 1)]

SCRATCH = dict(
    rows_in=((2, 9, 32, 256), BF),
    cols_out=((2, 80, 128), BF),
    cols_in=((6, 80, 128), BF),
    tile_out=((64, 128), BF),
    tiles_in=((20, 64, 128), BF),
    ext_side=((9, 96, 128), F32),
    ext=((9, 96, 384), BF),
    spread=((384, 512), BF),
    planar=((4, 16 * 96, 128), F32),
    rows_yc=((72, 16, 512), BF),
    eye=((160, 256), BF),
    fwin=((40, 160, 256), BF),
    s1=((36, 160, 128), BF),
    pix1=((34, 176, 128), F32),
    s2=((17, 80, 256), BF),
    pix2=((16, 112, 128), F32),
    s3=((5, 48, 512), BF),
    pix3o=((4, 48, 128), F32),
    pix3=((28, 112, 128), F32),
    s4=((11, 32, 512), BF),
    pix4=((10, 48, 128), F32),
    s5=((5, 16, 1024), BF),
    s6=((4, 16, 1024), BF),
    r7=((6, 32, 256), BF),
    k7=((6, 32, 512), BF),
    s8=((5, 32, 1024), BF),
    r9=((8, 48, 256), BF),
    k9=((8, 48, 512), BF),
    s10=((7, 48, 1024), BF),
    r11=((12, 80, 256), BF),
    k11=((12, 80, 256), BF),
    s12=((11, 80, 512), BF),
    r13=((24, 144, 128), BF),
    s14=((21, 144, 256), BF),
    s15=((20, 144, 128), BF),
    t128=((1928, 128), F32),
    t256=((1448, 256), F32),
    t512=((360, 512), F32),
    td=((20, 184, 128), F32),
    w15f=((32, 256), F32),
    flat=((16, 128), F32),
    table=((16, 512), F32),
    column=((16, 144), F32),
    z0=((144, 144), F32),
    z1=((144, 144), F32),
    zf=((2, 144, 128), F32),
    out32=((6, 32, 128), F32),
)
for _k in range(16):
    _n = 32 if _k == 15 else 256 if _k in SPLIT else 4 * NP[_k]
    SCRATCH["w%d" % _k] = ((KDIM[_k], _n) if _k in (0, 2, 3, 4, 5, 7, 9) else (_n, KDIM[_k]), BF)


def iota(shape, dim):
    return lax.broadcasted_iota(jnp.int32, shape, dim)


def nt(a, b):
    return lax.dot_general(a, b, (((1,), (1,)), ((), ())), preferred_element_type=F32)


FLIPPED = (0, 2, 3, 4, 5, 7, 9)


def tap_of(w, number, ky, kx, first, count):
    if number == 0:
        return w[ky, :, kx, :]
    if number in FLIPPED:
        return w[ky, kx, first : first + count, :]
    return w[ky, kx][:, first : first + count]


def put(wt, number, n, k, tap):
    if number in FLIPPED:
        wt[k : k + tap.shape[0], n : n + tap.shape[1]] = tap
    else:
        wt[n : n + tap.shape[0], k : k + tap.shape[1]] = tap


def prepare_blocks(wt, w, number, offset, first, count, lanes):
    for ky in range(3):
        for kx in range(3):
            tap = tap_of(w, number, ky, kx, first, count)
            for qy in range(2):
                for qx in range(2):
                    r, s = ky + qy, kx + qx
                    n = (qy * 2 + qx) * NP[number]
                    if number in SPLIT:
                        k = (r // 2 * 4 + r % 2 * 2 + s % 2) * lanes
                        n = n + s // 2 * 128
                    else:
                        k = offset + ((r // 2 * 2 + s // 2) * 4 + r % 2 * 2 + s % 2) * lanes
                    put(wt, number, n, k, tap)


def prepare_window(wt, w, number, offset, first):
    for ky in range(3):
        for kx in range(3):
            tap = tap_of(w, number, ky, kx, first, 9)
            for qy in range(2):
                for qx in range(2):
                    k = offset + (kx + qx) * 64 + (ky + qy) * 16
                    put(wt, number, (qy * 2 + qx) * NP[number], k, tap)


SUMS = {(0, 0): (0, 1), (0, 1): (2,), (1, 0): (0,), (1, 1): (1, 2)}


def prepare_up(wt, w, number, count, lanes):
    taps = [[tap_of(w, number, ky, kx, 0, count).astype(F32) for kx in range(3)] for ky in range(3)]
    for qy in range(2):
        for t in range(2):
            rows = SUMS[qy, t]
            line = taps[rows[0]] if len(rows) == 1 else [taps[rows[0]][kx] + taps[rows[1]][kx] for kx in range(3)]
            for qx in range(2):
                for u in range(2):
                    cols = SUMS[qx, u]
                    total = line[cols[0]] if len(cols) == 1 else line[cols[0]] + line[cols[1]]
                    put(wt, number, (qy * 2 + qx) * NP[number], (t * 2 + u) * lanes, total.astype(BF))


def prepare_biases(biases, flat, table, column):
    flat[...] = jnp.zeros(flat.shape, F32)
    for r in range(8):
        flat[r : r + 1, :] = biases[pl.ds(128 * r, 128)].reshape(1, 128)
    flat[8:9, 0:67] = biases[pl.ds(1024, 67)].reshape(1, 67)
    lane = iota((8, 128), 1)
    offset = 0
    for number in range(16):
        r, m = offset // 128, offset % 128
        offset = offset + COUT[number]
        pair = jnp.concatenate([flat[r : r + 1, :], flat[r + 1 : r + 2, :]], axis=1)
        pair = jnp.broadcast_to(pair, (8, 256))
        if m:
            pair = pltpu.roll(pair, 256 - m, 1)
        value = jnp.where(lane < COUT[number], pair[:, 0:128], 0.0)
        if number == 15:
            row = iota((16, 128), 0) % 8
            twice = jnp.concatenate([value, value], axis=0)
            mine = jnp.where((iota((16, 128), 1) == row % 3) & (row < 6), twice, 0.0)
            column[...] = jnp.broadcast_to(jnp.sum(mine, axis=1, keepdims=True), (16, 144))
            continue
        if NP[number] == 32:
            value = value + pltpu.roll(value, 32, 1)
        if NP[number] <= 64:
            value = value + pltpu.roll(value, 64, 1)
        for k in range(4 * NP[number] // 128):
            table[number : number + 1, 128 * k : 128 * k + 128] = value[0:1]


def kernel(sizes, feat, *refs):
    rows_ty, cols_tx = sizes
    sources = refs[:16]
    weights = refs[-17:-1]
    weight_sem = refs[-1]
    loads = [pltpu.make_async_copy(sources[k], weights[k], weight_sem.at[k]) for k in range(16)]
    for load in loads:
        load.start()
    out = refs[17]
    c = dict(zip(SCRATCH, refs[18 : 18 + len(SCRATCH)]))
    send1, recv1, send2, recv2 = refs[18 + len(SCRATCH) : 22 + len(SCRATCH)]
    table = c["table"]
    ty = lax.axis_index("ty")
    tx = lax.axis_index("tx")

    def device(dy, dx):
        return (ty + dy, tx + dx)

    def exists(dy, dx):
        found = None
        for here, step, size in ((ty, dy, rows_ty), (tx, dx, cols_tx)):
            if step:
                inside = here + step < size if step > 0 else here + step >= 0
                found = inside if found is None else found & inside
        return found

    def exchange(copies):
        for dy, dx, copy in copies:
            pl.when(exists(dy, dx))(copy.start)

        def wait():
            for dy, dx, copy in copies:
                pl.when(exists(dy, dx))(copy.wait_send)
                pl.when(exists(-dy, -dx))(copy.wait_recv)

        return wait

    barrier = pltpu.get_barrier_semaphore()
    for dy, dx in FAR:

        @pl.when(exists(dy, dx))
        def greet(dy=dy, dx=dx):
            pl.semaphore_signal(barrier, inc=1, device_id=device(dy, dx), device_id_type=MESH)


    lane9 = iota((9, 8, 128), 2)
    for side in range(2):
        value = jnp.zeros((9, 8, 128), F32)
        for g in range(4):
            piece = feat[:, 8 * g : 8 * g + 8, 128 * side : 128 * side + 128].astype(F32)
            shift = (32 * g - 96 * side) % 128
            if shift:
                piece = pltpu.roll(piece, shift, 2)
            value = jnp.where((lane9 >= 32 * g) & (lane9 < 32 * g + 32), piece, value)
        c["cols_out"][side, 0:72, :] = value.reshape(72, 128).astype(BF)
        c["cols_out"][side, 64:80, :] = jnp.concatenate(
            [value.reshape(72, 128)[64:72], jnp.zeros((8, 128), F32)], 0
        ).astype(BF)

    def clear(number):
        c["w%d" % number][...] = jnp.zeros(c["w%d" % number].shape, BF)

    for number in range(4):
        clear(number)
    for load in loads[:4]:
        load.wait()
    prepare_window(c["w0"], weights[0], 0, 0, 0)
    prepare_blocks(c["w1"], weights[1], 1, 0, 0, 32, 32)
    prepare_blocks(c["w2"], weights[2], 2, 0, 0, 32, 32)
    prepare_blocks(c["w3"], weights[3], 3, 0, 0, 48, 64)
    prepare_biases(refs[16], c["flat"], c["table"], c["column"])

    place = iota((384, 128), 0)
    x = jnp.where(place < 256, place, jnp.where(place < 288, place - 288, jnp.where(place < 320, place - 32, -1000)))
    x = x - 2 * iota((384, 128), 1) + 36
    for px in range(2):
        for half in range(2):
            hit = jnp.where(x == px + 256 * half, 1.0, 0.0)
            c["spread"][:, 256 * px + 128 * half : 256 * px + 128 * half + 128] = hit.astype(BF)
    c["eye"][...] = (iota((160, 256), 0) == iota((160, 256), 1)).astype(F32).astype(BF)
    for k in range(4):
        c["planar"][k, 864:1536, :] = jnp.zeros((672, 128), F32)

    def reach(here, size, most):
        total = 1
        for k in range(1, most + 1):
            total = total + lax.div(here + size - k, size) + 1 - lax.div(here + k, size)
        return total

    pl.semaphore_wait(barrier, reach(ty, rows_ty, 3) * reach(tx, cols_tx, 1) - 1)
    copies = []
    for number, (dy, dx) in enumerate(DIRS):
        if dx == 0:
            source, target = feat, c["rows_in"].at[0 if dy == 1 else 1]
        else:
            source = c["cols_out"].at[0 if dx == -1 else 1]
            target = c["cols_in"].at[(0 if dx == -1 else 3) + dy + 1]
        copy = pltpu.make_async_remote_copy(
            src_ref=source,
            dst_ref=target,
            send_sem=send1.at[number],
            recv_sem=recv1.at[number],
            device_id=device(dy, dx),
            device_id_type=MESH,
        )
        copies.append((dy, dx, copy))

    wait = exchange(copies)

    for number in range(4, 15):
        clear(number)
    for load in loads[4:]:
        load.wait()
    prepare_blocks(c["w4"], weights[4], 4, 0, 0, 64, 64)
    prepare_blocks(c["w5"], weights[5], 5, 0, 0, 80, 128)
    prepare_blocks(c["w6"], weights[6], 6, 0, 0, 96, 128)
    prepare_up(c["w7"], weights[7], 7, 96, 128)
    prepare_blocks(c["w7"], weights[7], 7, 512, 96, 64, 64)
    prepare_blocks(c["w8"], weights[8], 8, 0, 0, 112, 128)
    prepare_up(c["w9"], weights[9], 9, 112, 128)
    prepare_blocks(c["w9"], weights[9], 9, 512, 112, 48, 64)
    prepare_blocks(c["w10"], weights[10], 10, 0, 0, 96, 128)
    prepare_up(c["w11"], weights[11], 11, 96, 128)
    prepare_blocks(c["w11"], weights[11], 11, 512, 96, 32, 32)
    prepare_blocks(c["w12"], weights[12], 12, 0, 0, 64, 64)
    prepare_up(c["w13"], weights[13], 13, 64, 64)
    prepare_window(c["w13"], weights[13], 13, 256, 64)
    prepare_blocks(c["w14"], weights[14], 14, 0, 0, 64, 64)
    c["w15f"][...] = jnp.zeros((32, 256), F32)
    for ky in range(3):
        for kx in range(3):
            tap = weights[15][ky, kx].astype(F32)
            for qy in range(2):
                for qx in range(2):
                    r, s = ky + qy, kx + qx
                    k = (r // 2 * 4 + r % 2 * 2 + s % 2) * 32
                    n = s // 2 * 16 + qx * 8 + qy * 3
                    c["w15f"][n : n + 3, k : k + 32] = tap
    c["w15"][...] = c["w15f"][...].astype(BF)
    wait()

    first_row = jnp.where(ty > 0, 1.0, 0.0)
    last_row = jnp.where(ty < rows_ty - 1, 1.0, 0.0)
    first_col = jnp.where(tx > 0, 1.0, 0.0)
    last_col = jnp.where(tx < cols_tx - 1, 1.0, 0.0)
    c["ext"][:, 0:32, 0:256] = jnp.where(first_row > 0, c["rows_in"][0].astype(F32), 0.0).astype(BF)
    c["ext"][:, 32:64, 0:256] = feat[...]
    c["ext"][:, 64:96, 0:256] = jnp.where(last_row > 0, c["rows_in"][1].astype(F32), 0.0).astype(BF)
    for k in range(3):
        row_ok = (first_row, 1.0, last_row)[k]
        left = c["cols_in"][3 + (1, 0, -1)[k] + 1].astype(F32)[0:72].reshape(9, 8, 128)
        right = c["cols_in"][(1, 0, -1)[k] + 1].astype(F32)[0:72].reshape(9, 8, 128)
        left = jnp.where(row_ok * first_col > 0, left, 0.0)
        right = jnp.where(row_ok * last_col > 0, right, 0.0)
        for g in range(4):
            to_left = pltpu.roll(left, (128 - 32 * g) % 128, 2) if g else left
            to_right = pltpu.roll(right, (160 - 32 * g) % 128, 2) if g != 1 else right
            piece = jnp.where(lane9 < 32, to_left, jnp.where(lane9 < 64, to_right, 0.0))
            c["ext_side"][:, 32 * k + 8 * g : 32 * k + 8 * g + 8, :] = piece
    c["ext"][:, :, 256:384] = c["ext_side"][...].astype(BF)

    def spread_channel(ch, _):
        wide = jnp.dot(c["ext"][ch], c["spread"][...], preferred_element_type=F32)
        for k in range(4):
            c["planar"][k, pl.ds(pl.multiple_of(ch * 96, 96), 96), :] = wide[:, 128 * k : 128 * k + 128]
        return 0

    lax.fori_loop(0, 9, spread_channel, 0, unroll=3)

    def gather_row(y, _):
        for k in range(4):
            c["rows_yc"][y, :, 128 * k : 128 * k + 128] = c["planar"][k, pl.ds(y + 12, 16, stride=96), :].astype(BF)
        return 0

    lax.fori_loop(0, 72, gather_row, 0, unroll=4)

    def column_cap(number, first, count, origin, width):
        np_ = NP[number]
        n = 4 * np_
        at = origin + 2 * (first + iota((count, n), 0)) + (iota((count, n), 1) // np_) % 2 + tx * width
        return jnp.where((at >= 0) & (at < width * cols_tx), BIG, 0.0)

    def edges(wp, origin, width):
        low = (-(origin // 2) + 7) // 8 * 8
        return low, min((width - origin) // 2 // 8 * 8, wp)

    def finish(number, r, caps, i0, g, wp, origin_y, origin_x, height, width):
        np_ = NP[number]
        n = 4 * np_
        u = jnp.maximum(r + table[number : number + 1, 0:n], 0.0)
        low, high = edges(wp, origin_x, width)
        pieces = []
        for k in range(g):
            v = u[k * wp : (k + 1) * wp]
            parts = [jnp.minimum(v[0:low], caps[0])] if low else []
            parts = parts + ([v[low:high]] if high > low else [])
            parts = parts + ([jnp.minimum(v[high:wp], caps[1])] if wp > high else [])
            v = jnp.concatenate(parts, axis=0) if len(parts) > 1 else parts[0]
            y = origin_y + 2 * (i0 + k)
            if y < 0 or y + 2 > height:
                at = y + iota((1, n), 1) // (2 * np_) + ty * height
                v = jnp.minimum(v, jnp.where((at >= 0) & (at < height * rows_ty), BIG, 0.0))
            pieces.append(v)
        return pieces

    def to_blocks(pieces, target, i0, wp, n):
        t = c["t%d" % n]
        g = len(pieces)
        if target.shape[2] == n:
            for k in range(g):
                target[i0 + k, :, :] = pieces[k].astype(BF)
            return
        for k in range(g):
            t[k * wp : (k + 1) * wp, :] = pieces[k]
            target[i0 + k, :, 0:n] = pieces[k].astype(BF)
        for k in range(g):
            target[i0 + k, :, n : 2 * n] = t[k * wp + 1 : (k + 1) * wp + 1, :].astype(BF)

    def pooled(piece, np_):
        if np_ == 32:
            m = jnp.maximum(piece, pltpu.roll(piece, 64, 1))
            return jnp.maximum(m, pltpu.roll(m, 32, 1))
        if np_ == 64:
            m = jnp.maximum(piece[:, 0:128], piece[:, 128:256])
            return jnp.maximum(m, pltpu.roll(m, 64, 1))
        m = jnp.maximum(piece[:, 0:128], piece[:, 128:256])
        return jnp.maximum(m, jnp.maximum(piece[:, 256:384], piece[:, 384:512]))

    def pack(pixels, target, first, count, wp, lanes, row0, col0):
        lane = iota((wp, 128), 1)

        def step(i, _):
            a = [
                [pixels[row0 + 2 * i + py, pl.ds(col0 + m, wp, stride=2), :] for m in range(4)] for py in range(2)
            ]
            for u in range(2):
                four = [a[0][2 * u], a[0][2 * u + 1], a[1][2 * u], a[1][2 * u + 1]]
                base = u * 4 * lanes
                if lanes == 32:
                    v = jnp.where(
                        lane < 64,
                        jnp.where(lane < 32, four[0], four[1]),
                        jnp.where(lane < 96, four[2], four[3]),
                    )
                    target[i, :, base : base + 128] = v.astype(BF)
                elif lanes == 64:
                    for py in range(2):
                        v = jnp.where(lane < 64, four[2 * py], four[2 * py + 1])
                        target[i, :, base + 128 * py : base + 128 * py + 128] = v.astype(BF)
                else:
                    for q in range(4):
                        target[i, :, base + 128 * q : base + 128 * q + 128] = four[q].astype(BF)
            return 0

        lax.fori_loop(first, first + count, step, 0, unroll=True)

    def to_pixels(pieces, target, i0, wp, wr, np_):
        td = c["td"]
        lane = iota((wp, 128), 1)
        lane_r = iota((wr, 128), 1)
        for k in range(len(pieces)):
            for qy in range(2):
                at = 2 * k + qy
                if np_ == 128:
                    even = pieces[k][:, 256 * qy : 256 * qy + 128]
                    odd = pieces[k][:, 256 * qy + 128 : 256 * qy + 256]
                else:
                    v = pieces[k][:, 128 * qy : 128 * qy + 128]
                    w = pltpu.roll(v, 64, 1)
                    even = jnp.where(lane < 64, v, w)
                    odd = jnp.where(lane < 64, w, v)
                td[at, pl.ds(0, wp, stride=2), :] = even
                td[at, pl.ds(1, wp, stride=2), :] = odd
        for k in range(len(pieces)):
            for qy in range(2):
                at = 2 * k + qy
                here, right = td[at, 0:wr, :], td[at, 1 : wr + 1, :]
                if np_ == 128:
                    target[2 * (i0 + k) + qy, :, 0:128] = here.astype(BF)
                    target[2 * (i0 + k) + qy, :, 128:256] = right.astype(BF)
                else:
                    target[2 * (i0 + k) + qy, :, :] = jnp.where(lane_r < 64, here, right).astype(BF)

    def block_input(ref):
        def load(i0, g):
            lanes = ref.shape[2]
            rows = g * ref.shape[1]
            return [
                ref[pl.ds(i0, g)].reshape(rows, lanes),
                ref[pl.ds(i0 + 1, g)].reshape(rows, lanes),
            ]

        return load

    def layer(number, loads, first, count, g, wp, origin_y, origin_x, level, store):
        height, width = 32 >> level, 256 >> level
        low, high = edges(wp, origin_x, width)
        caps = (
            column_cap(number, 0, low, origin_x, width) if low else None,
            column_cap(number, high, wp - high, origin_x, width) if wp > high else None,
        )

        def step(it, _):
            i0 = first + it * g
            lhs = []
            for load in loads:
                lhs = lhs + load(i0, g)
            lhs = jnp.concatenate(lhs, axis=1) if len(lhs) > 1 else lhs[0]
            if number in FLIPPED:
                r = jnp.dot(lhs, c["w%d" % number][...], preferred_element_type=F32)
            else:
                r = nt(lhs, c["w%d" % number][...])
            if number in SPLIT:
                c["t128"][0 : g * wp, :] = r[:, 128:256]
                r = r[:, 0:128] + c["t128"][1 : g * wp + 1, :]
            store(finish(number, r, caps, i0, g, wp, origin_y, origin_x, height, width), i0)
            return 0

        for it in range(count):
            step(it, 0)

    def pool_into(pixels, number, wp):
        def store(pieces, i0):
            for k, piece in enumerate(pieces):
                pixels[i0 + k, 0:wp, :] = pooled(piece, NP[number])

        return store

    def windows(first, count, g):
        t = c["t128"]

        def step(it, _):
            i0 = first + it * g
            for k in range(g):
                rows = c["rows_yc"][pl.ds(2 * (i0 + k), 4)].reshape(64, 512)
                stacked = jnp.concatenate([rows[:, 0:256], rows[:, 256:512]], axis=0)
                turned = nt(c["eye"][...], stacked)
                c["fwin"][i0 + k, :, 0:128] = turned.astype(BF)
                t[k * 160 : (k + 1) * 160, :] = turned
            for k in range(g):
                c["fwin"][i0 + k, :, 128:256] = t[k * 160 + 1 : (k + 1) * 160 + 1, :].astype(BF)
            return 0

        if count == 1:
            step(0, 0)
        else:
            lax.fori_loop(0, count, step, 0)

    def window_load(i0, g):
        return [c["fwin"][pl.ds(i0, g)].reshape(g * 160, 256)]

    def conv0(first, count, g):
        layer(0, [window_load], first, count, g, 160, -19, -35, 0, lambda p, i0: to_blocks(p, c["s1"], i0, 160, 128))

    def conv1(first, count, g):
        layer(1, [block_input(c["s1"])], first, count, g, 160, -18, -34, 0, pool_into(c["pix1"], 1, 160))

    def conv2(first, count, g):
        layer(2, [block_input(c["s2"])], first, count, g, 80, -8, -8, 1, pool_into(c["pix2"], 2, 80))

    windows(6, 2, 12)
    conv0(6, 2, 12)
    conv1(6, 2, 11)
    pack(c["pix1"], c["s2"], 3, 11, 80, 32, 0, 8)
    conv2(3, 1, 10)
    pack(c["pix2"], c["s3"], 0, 5, 48, 64, 3, 3)
    layer(3, [block_input(c["s3"])], 0, 1, 4, 48, 0, 0, 2, pool_into(c["pix3o"], 3, 48))

    lane8 = iota((8, 128), 1)
    pieces = []
    for half in range(2):
        for y in range(4):
            even = c["pix3o"][y, pl.ds(16 * half, 8, stride=2), :]
            odd = c["pix3o"][y, pl.ds(16 * half + 1, 8, stride=2), :]
            pieces.append(jnp.where(lane8 < 64, even, odd))
    c["tile_out"][...] = jnp.concatenate(pieces, axis=0).astype(BF)
    copies = []
    for number, (dy, dx) in enumerate(FAR):
        rows = pl.ds(0, 64) if dx == 0 else pl.ds(32, 32) if dx == 1 else pl.ds(0, 32)
        copy = pltpu.make_async_remote_copy(
            src_ref=c["tile_out"].at[rows],
            dst_ref=c["tiles_in"].at[number, rows],
            send_sem=send2.at[number],
            recv_sem=recv2.at[number],
            device_id=device(dy, dx),
            device_id_type=MESH,
        )
        copies.append((dy, dx, copy))

    wait = exchange(copies)

    windows(0, 1, 6)
    windows(30, 1, 5)
    conv0(0, 1, 6)
    conv0(30, 1, 5)
    conv1(0, 1, 6)
    conv1(28, 1, 6)
    pack(c["pix1"], c["s2"], 0, 3, 80, 32, 0, 8)
    pack(c["pix1"], c["s2"], 14, 3, 80, 32, 0, 8)
    conv2(0, 1, 3)
    conv2(13, 1, 3)
    pack(c["pix1"], c["k11"], 0, 12, 80, 32, 5, 13)
    pack(c["pix2"], c["k9"], 0, 8, 48, 64, 0, 0)

    wait()

    slot = {d: n for n, d in enumerate(FAR)}
    for ky in range(-3, 4):
        for kx in range(-1, 2):
            if (ky, kx) == (0, 0):
                tile = c["tile_out"][...].astype(F32)
            else:
                ok = (ty + ky >= 0) & (ty + ky < rows_ty) & (tx + kx >= 0) & (tx + kx < cols_tx)
                tile = jnp.where(jnp.where(ok, 1.0, 0.0) > 0, c["tiles_in"][slot[-ky, -kx]].astype(F32), 0.0)
            halves = (0, 1) if kx == 0 else (1,) if kx == -1 else (0,)
            for y in range(4):
                if ky == -3 and y < 3 or ky == 3 and y > 0:
                    continue
                for half in halves:
                    v = tile[32 * half + 8 * y : 32 * half + 8 * y + 8]
                    w = pltpu.roll(v, 64, 1)
                    row = 12 + 4 * ky + y
                    col = 32 * (kx + 1) + 16 * half
                    c["pix3"][row, pl.ds(col, 8, stride=2), :] = jnp.where(lane8 < 64, v, w)
                    c["pix3"][row, pl.ds(col + 1, 8, stride=2), :] = jnp.where(lane8 < 64, w, v)

    pack(c["pix3"], c["s4"], 0, 11, 32, 64, 3, 23)
    pack(c["pix3"], c["k7"], 0, 6, 32, 64, 8, 28)

    layer(4, [block_input(c["s4"])], 0, 1, 10, 32, -8, -8, 3, pool_into(c["pix4"], 4, 32))
    pack(c["pix4"], c["s5"], 0, 5, 16, 128, 0, 0)
    layer(5, [block_input(c["s5"])], 0, 1, 4, 16, -3, -3, 4, lambda p, i0: to_blocks(p, c["s6"], i0, 16, 512))
    layer(6, [block_input(c["s6"])], 0, 1, 3, 16, -2, -2, 4, lambda p, i0: to_pixels(p, c["r7"], i0, 16, 32, 128))
    layer(
        7, [block_input(c["r7"]), block_input(c["k7"])], 0, 1, 5, 32, -3, -3, 3,
        lambda p, i0: to_blocks(p, c["s8"], i0, 32, 512),
    )
    layer(8, [block_input(c["s8"])], 0, 1, 4, 32, -2, -2, 3, lambda p, i0: to_pixels(p, c["r9"], i0, 32, 48, 128))
    layer(
        9, [block_input(c["r9"]), block_input(c["k9"])], 0, 1, 7, 48, -3, -3, 2,
        lambda p, i0: to_blocks(p, c["s10"], i0, 48, 512),
    )
    layer(10, [block_input(c["s10"])], 0, 1, 6, 48, -2, -2, 2, lambda p, i0: to_pixels(p, c["r11"], i0, 48, 80, 128))
    layer(
        11, [block_input(c["r11"]), block_input(c["k11"])], 0, 1, 11, 80, -3, -3, 1,
        lambda p, i0: to_blocks(p, c["s12"], i0, 80, 256),
    )
    layer(12, [block_input(c["s12"])], 0, 1, 10, 80, -2, -2, 1, lambda p, i0: to_pixels(p, c["r13"], i0, 80, 144, 64))

    def features_load(i0, g):
        return [c["fwin"][pl.ds(i0 + 8, g), 16:160, :].reshape(g * 144, 256)]

    layer(
        13, [block_input(c["r13"]), features_load], 0, 1, 10, 144, -3, -3, 0,
        lambda p, i0: to_blocks(p, c["s14"], i0, 144, 256),
    )
    layer(
        13, [block_input(c["r13"]), features_load], 10, 1, 9, 144, -3, -3, 0,
        lambda p, i0: to_blocks(p, c["s14"], i0, 144, 256),
    )
    layer(14, [block_input(c["s14"])], 0, 2, 9, 144, -2, -2, 0, lambda p, i0: to_blocks(p, c["s15"], i0, 144, 128))

    lane144 = iota((16, 144), 1)

    def last(i, _):
        field = jnp.concatenate([c["s15"][i], c["s15"][i + 1]], axis=1)
        r = nt(c["w15"][...], field)
        r = r[0:16] + pltpu.roll(r[16:32], 143, 1) + c["column"][...]
        r = jnp.where(lane144 < 129, r, 0.0)
        c["z0"][pl.ds(pl.multiple_of(8 * i, 8), 8), :] = r[0:8]
        c["z1"][pl.ds(pl.multiple_of(8 * i, 8), 8), :] = r[8:16]
        return 0

    c["z0"][136:144, :] = jnp.zeros((8, 144), F32)
    c["z1"][136:144, :] = jnp.zeros((8, 144), F32)
    lax.fori_loop(0, 17, last, 0, unroll=17)
    at = iota((144, 256), 1) - 2 * iota((144, 256), 0)
    even = (at == -1).astype(F32).astype(BF)
    odd = (at == 0).astype(F32).astype(BF)
    wide = jnp.dot(c["z0"][...].astype(BF), even, preferred_element_type=F32) + jnp.dot(
        c["z1"][...].astype(BF), odd, preferred_element_type=F32
    )
    for half in range(2):
        lanes = slice(128 * half, 128 * half + 128)
        c["zf"][half] = wide[:, lanes]
        for o in range(3):
            c["out32"][2 * o + half, pl.ds(0, 16, stride=2), :] = c["zf"][half, pl.ds(3 + o, 16, stride=8), :]
            c["out32"][2 * o + half, pl.ds(1, 16, stride=2), :] = c["zf"][half, pl.ds(8 + o, 16, stride=8), :]
            out[o, :, lanes] = c["out32"][2 * o + half].astype(BF)


def body(sizes, features, *rest):
    weights, biases = list(rest[:16]), rest[16]
    for number in FLIPPED:
        weights[number] = jnp.transpose(weights[number], (0, 1, 3, 2) if number else (0, 3, 1, 2))
    vmem = pl.BlockSpec(memory_space=pltpu.VMEM)
    scratch = [pltpu.VMEM(shape, kind) for shape, kind in SCRATCH.values()]
    scratch += [pltpu.SemaphoreType.DMA((n,)) for n in (8, 8, 20, 20)]
    scratch += [pltpu.VMEM(w.shape, BF) for w in weights] + [pltpu.SemaphoreType.DMA((16,))]
    return pl.pallas_call(
        functools.partial(kernel, sizes),
        out_shape=jax.ShapeDtypeStruct((3, 32, 256), BF),
        in_specs=[vmem] + [pl.BlockSpec(memory_space=pl.ANY)] * 16 + [vmem],
        out_specs=vmem,
        scratch_shapes=scratch,
        compiler_params=pltpu.CompilerParams(
            collective_id=0, has_side_effects=True, vmem_limit_bytes=58 << 20
        ),
    )(features, *weights, biases)


def solution(mesh):
    sizes = (mesh.shape["ty"], mesh.shape["tx"])
    return jax.shard_map(
        functools.partial(body, sizes),
        mesh=mesh,
        in_specs=(P(None, "ty", "tx"),) + (P(),) * 17,
        out_specs=P(None, "ty", "tx"),
        check_vma=False,
    )
```

```python
import functools

import jax
import jax.numpy as jnp
from jax import lax
from jax.experimental import pallas as pl
from jax.experimental.pallas import tpu as pltpu
from jax.sharding import PartitionSpec as P

F32 = jnp.float32
BF = jnp.bfloat16
BIG = 3.0e38
MESH = pl.DeviceIdType.MESH

COUT = [32, 32, 48, 64, 80, 96, 96, 112, 112, 96, 96, 64, 64, 64, 32, 3]
CIN = [9, 32, 32, 48, 64, 80, 96, 160, 112, 160, 96, 128, 64, 73, 64, 32]
NP = [32, 32, 64, 64, 128, 128, 128, 128, 128, 128, 128, 64, 64, 64, 32, 4]
KDIM = [256, 256, 512, 1024, 1024, 2048, 2048, 1536, 2048, 1536, 2048, 1024, 1024, 512, 512, 256]
SPLIT = (1, 14, 15)
DIRS = [(dy, dx) for dy in (-1, 0, 1) for dx in (-1, 0, 1) if (dy, dx) != (0, 0)]
FAR = DIRS + [(dy, dx) for dy in (-3, -2, 2, 3) for dx in (-1, 0, 1)]

SCRATCH = dict(
    rows_in=((2, 9, 32, 256), BF),
    cols_out=((2, 80, 128), BF),
    cols_in=((6, 80, 128), BF),
    tile_out=((64, 128), BF),
    tiles_in=((20, 64, 128), BF),
    ext_side=((9, 96, 128), F32),
    ext=((9, 96, 384), BF),
    spread=((384, 512), BF),
    planar=((4, 16 * 96, 128), F32),
    rows_yc=((72, 16, 512), BF),
    eye=((160, 256), BF),
    fwin=((40, 160, 256), BF),
    s1=((36, 160, 128), BF),
    pix1=((34, 176, 128), F32),
    s2=((17, 80, 256), BF),
    pix2=((16, 112, 128), F32),
    s3=((5, 48, 512), BF),
    pix3o=((4, 48, 128), F32),
    pix3=((28, 112, 128), F32),
    s4=((11, 32, 512), BF),
    pix4=((10, 48, 128), F32),
    s5=((5, 16, 1024), BF),
    s6=((4, 16, 1024), BF),
    r7=((6, 32, 256), BF),
    k7=((6, 32, 512), BF),
    s8=((5, 32, 1024), BF),
    r9=((8, 48, 256), BF),
    k9=((8, 48, 512), BF),
    s10=((7, 48, 1024), BF),
    r11=((12, 80, 256), BF),
    k11=((12, 80, 256), BF),
    s12=((11, 80, 512), BF),
    r13=((24, 144, 128), BF),
    s14=((21, 144, 256), BF),
    s15=((20, 144, 128), BF),
    t128=((1928, 128), F32),
    t256=((1448, 256), F32),
    t512=((360, 512), F32),
    td=((20, 184, 128), F32),
    w15f=((32, 256), F32),
    flat=((16, 128), F32),
    table=((16, 512), F32),
    column=((16, 144), F32),
    z0=((144, 144), F32),
    z1=((144, 144), F32),
    zf=((2, 144, 128), F32),
    out32=((6, 32, 128), F32),
)
for _k in range(16):
    _n = 32 if _k == 15 else 256 if _k in SPLIT else 4 * NP[_k]
    SCRATCH["w%d" % _k] = ((KDIM[_k], _n) if _k in (0, 2, 3, 4, 5, 7, 9) else (_n, KDIM[_k]), BF)


def iota(shape, dim):
    return lax.broadcasted_iota(jnp.int32, shape, dim)


def nt(a, b):
    return lax.dot_general(a, b, (((1,), (1,)), ((), ())), preferred_element_type=F32)


FLIPPED = (0, 2, 3, 4, 5, 7, 9)


def tap_of(w, number, ky, kx, first, count):
    if number == 0:
        return w[ky, :, kx, :]
    if number in FLIPPED:
        return w[ky, kx, first : first + count, :]
    return w[ky, kx][:, first : first + count]


def put(wt, number, n, k, tap):
    if number in FLIPPED:
        wt[k : k + tap.shape[0], n : n + tap.shape[1]] = tap
    else:
        wt[n : n + tap.shape[0], k : k + tap.shape[1]] = tap


def prepare_blocks(wt, w, number, offset, first, count, lanes):
    for ky in range(3):
        for kx in range(3):
            tap = tap_of(w, number, ky, kx, first, count)
            for qy in range(2):
                for qx in range(2):
                    r, s = ky + qy, kx + qx
                    n = (qy * 2 + qx) * NP[number]
                    if number in SPLIT:
                        k = (r // 2 * 4 + r % 2 * 2 + s % 2) * lanes
                        n = n + s // 2 * 128
                    else:
                        k = offset + ((r // 2 * 2 + s // 2) * 4 + r % 2 * 2 + s % 2) * lanes
                    put(wt, number, n, k, tap)


def prepare_window(wt, w, number, offset, first):
    for ky in range(3):
        for kx in range(3):
            tap = tap_of(w, number, ky, kx, first, 9)
            for qy in range(2):
                for qx in range(2):
                    k = offset + (kx + qx) * 64 + (ky + qy) * 16
                    put(wt, number, (qy * 2 + qx) * NP[number], k, tap)


SUMS = {(0, 0): (0, 1), (0, 1): (2,), (1, 0): (0,), (1, 1): (1, 2)}


def prepare_up(wt, w, number, count, lanes):
    taps = [[tap_of(w, number, ky, kx, 0, count).astype(F32) for kx in range(3)] for ky in range(3)]
    for qy in range(2):
        for t in range(2):
            rows = SUMS[qy, t]
            line = taps[rows[0]] if len(rows) == 1 else [taps[rows[0]][kx] + taps[rows[1]][kx] for kx in range(3)]
            for qx in range(2):
                for u in range(2):
                    cols = SUMS[qx, u]
                    total = line[cols[0]] if len(cols) == 1 else line[cols[0]] + line[cols[1]]
                    put(wt, number, (qy * 2 + qx) * NP[number], (t * 2 + u) * lanes, total.astype(BF))


def prepare_biases(biases, flat, table, column):
    flat[...] = jnp.zeros(flat.shape, F32)
    for r in range(8):
        flat[r : r + 1, :] = biases[pl.ds(128 * r, 128)].reshape(1, 128)
    flat[8:9, 0:67] = biases[pl.ds(1024, 67)].reshape(1, 67)
    lane = iota((8, 128), 1)
    offset = 0
    for number in range(16):
        r, m = offset // 128, offset % 128
        offset = offset + COUT[number]
        pair = jnp.concatenate([flat[r : r + 1, :], flat[r + 1 : r + 2, :]], axis=1)
        pair = jnp.broadcast_to(pair, (8, 256))
        if m:
            pair = pltpu.roll(pair, 256 - m, 1)
        value = jnp.where(lane < COUT[number], pair[:, 0:128], 0.0)
        if number == 15:
            row = iota((16, 128), 0) % 8
            twice = jnp.concatenate([value, value], axis=0)
            mine = jnp.where((iota((16, 128), 1) == row % 3) & (row < 6), twice, 0.0)
            column[...] = jnp.broadcast_to(jnp.sum(mine, axis=1, keepdims=True), (16, 144))
            continue
        if NP[number] == 32:
            value = value + pltpu.roll(value, 32, 1)
        if NP[number] <= 64:
            value = value + pltpu.roll(value, 64, 1)
        for k in range(4 * NP[number] // 128):
            table[number : number + 1, 128 * k : 128 * k + 128] = value[0:1]


def kernel(sizes, feat, *refs):
    rows_ty, cols_tx = sizes
    sources = refs[:16]
    weights = refs[-17:-1]
    weight_sem = refs[-1]
    loads = [pltpu.make_async_copy(sources[k], weights[k], weight_sem.at[k]) for k in range(16)]
    out = refs[17]
    c = dict(zip(SCRATCH, refs[18 : 18 + len(SCRATCH)]))
    send1, recv1, send2, recv2 = refs[18 + len(SCRATCH) : 22 + len(SCRATCH)]
    table = c["table"]
    ty = lax.axis_index("ty")
    tx = lax.axis_index("tx")

    def device(dy, dx):
        return (ty + dy, tx + dx)

    def exists(dy, dx):
        found = None
        for here, step, size in ((ty, dy, rows_ty), (tx, dx, cols_tx)):
            if step:
                inside = here + step < size if step > 0 else here + step >= 0
                found = inside if found is None else found & inside
        return found

    def exchange(copies):
        for dy, dx, copy in sorted(copies, key=lambda c: c[1] == 0):
            pl.when(exists(dy, dx))(copy.start)

        def wait():
            for dy, dx, copy in copies:
                pl.when(exists(dy, dx))(copy.wait_send)
                pl.when(exists(-dy, -dx))(copy.wait_recv)

        return wait

    barrier = pltpu.get_barrier_semaphore()
    for dy, dx in sorted(FAR, key=lambda d: d[1] == 0):

        @pl.when(exists(dy, dx))
        def greet(dy=dy, dx=dx):
            pl.semaphore_signal(barrier, inc=1, device_id=device(dy, dx), device_id_type=MESH)


    for load in loads:
        load.start()

    lane9 = iota((9, 8, 128), 2)
    for side in range(2):
        value = jnp.zeros((9, 8, 128), F32)
        for g in range(4):
            piece = feat[:, 8 * g : 8 * g + 8, 128 * side : 128 * side + 128].astype(F32)
            shift = (32 * g - 96 * side) % 128
            if shift:
                piece = pltpu.roll(piece, shift, 2)
            value = jnp.where((lane9 >= 32 * g) & (lane9 < 32 * g + 32), piece, value)
        c["cols_out"][side, 0:72, :] = value.reshape(72, 128).astype(BF)
        c["cols_out"][side, 64:80, :] = jnp.concatenate(
            [value.reshape(72, 128)[64:72], jnp.zeros((8, 128), F32)], 0
        ).astype(BF)

    def clear(number):
        c["w%d" % number][...] = jnp.zeros(c["w%d" % number].shape, BF)

    for number in range(4):
        clear(number)
    for load in loads[:4]:
        load.wait()
    prepare_window(c["w0"], weights[0], 0, 0, 0)
    prepare_blocks(c["w1"], weights[1], 1, 0, 0, 32, 32)
    prepare_blocks(c["w2"], weights[2], 2, 0, 0, 32, 32)
    prepare_blocks(c["w3"], weights[3], 3, 0, 0, 48, 64)
    prepare_biases(refs[16], c["flat"], c["table"], c["column"])

    place = iota((384, 128), 0)
    x = jnp.where(place < 256, place, jnp.where(place < 288, place - 288, jnp.where(place < 320, place - 32, -1000)))
    x = x - 2 * iota((384, 128), 1) + 36
    for px in range(2):
        for half in range(2):
            hit = jnp.where(x == px + 256 * half, 1.0, 0.0)
            c["spread"][:, 256 * px + 128 * half : 256 * px + 128 * half + 128] = hit.astype(BF)
    c["eye"][...] = (iota((160, 256), 0) == iota((160, 256), 1)).astype(F32).astype(BF)
    for k in range(4):
        c["planar"][k, 864:1536, :] = jnp.zeros((672, 128), F32)

    def reach(here, size, most):
        total = 1
        for k in range(1, most + 1):
            total = total + lax.div(here + size - k, size) + 1 - lax.div(here + k, size)
        return total

    pl.semaphore_wait(barrier, reach(ty, rows_ty, 3) * reach(tx, cols_tx, 1) - 1)
    copies = []
    for number, (dy, dx) in enumerate(DIRS):
        if dx == 0:
            source, target = feat, c["rows_in"].at[0 if dy == 1 else 1]
        else:
            source = c["cols_out"].at[0 if dx == -1 else 1]
            target = c["cols_in"].at[(0 if dx == -1 else 3) + dy + 1]
        copy = pltpu.make_async_remote_copy(
            src_ref=source,
            dst_ref=target,
            send_sem=send1.at[number],
            recv_sem=recv1.at[number],
            device_id=device(dy, dx),
            device_id_type=MESH,
        )
        copies.append((dy, dx, copy))

    wait = exchange(copies)

    for number in range(4, 15):
        clear(number)
    for load in loads[4:]:
        load.wait()
    prepare_blocks(c["w4"], weights[4], 4, 0, 0, 64, 64)
    prepare_blocks(c["w5"], weights[5], 5, 0, 0, 80, 128)
    prepare_blocks(c["w6"], weights[6], 6, 0, 0, 96, 128)
    prepare_up(c["w7"], weights[7], 7, 96, 128)
    prepare_blocks(c["w7"], weights[7], 7, 512, 96, 64, 64)
    prepare_blocks(c["w8"], weights[8], 8, 0, 0, 112, 128)
    prepare_up(c["w9"], weights[9], 9, 112, 128)
    prepare_blocks(c["w9"], weights[9], 9, 512, 112, 48, 64)
    prepare_blocks(c["w10"], weights[10], 10, 0, 0, 96, 128)
    prepare_up(c["w11"], weights[11], 11, 96, 128)
    prepare_blocks(c["w11"], weights[11], 11, 512, 96, 32, 32)
    prepare_blocks(c["w12"], weights[12], 12, 0, 0, 64, 64)
    prepare_up(c["w13"], weights[13], 13, 64, 64)
    prepare_window(c["w13"], weights[13], 13, 256, 64)
    prepare_blocks(c["w14"], weights[14], 14, 0, 0, 64, 64)
    c["w15f"][...] = jnp.zeros((32, 256), F32)
    for ky in range(3):
        for kx in range(3):
            tap = weights[15][ky, kx].astype(F32)
            for qy in range(2):
                for qx in range(2):
                    r, s = ky + qy, kx + qx
                    k = (r // 2 * 4 + r % 2 * 2 + s % 2) * 32
                    n = s // 2 * 16 + qx * 8 + qy * 3
                    c["w15f"][n : n + 3, k : k + 32] = tap
    c["w15"][...] = c["w15f"][...].astype(BF)
    wait()

    first_row = jnp.where(ty > 0, 1.0, 0.0)
    last_row = jnp.where(ty < rows_ty - 1, 1.0, 0.0)
    first_col = jnp.where(tx > 0, 1.0, 0.0)
    last_col = jnp.where(tx < cols_tx - 1, 1.0, 0.0)
    c["ext"][:, 0:32, 0:256] = jnp.where(first_row > 0, c["rows_in"][0].astype(F32), 0.0).astype(BF)
    c["ext"][:, 32:64, 0:256] = feat[...]
    c["ext"][:, 64:96, 0:256] = jnp.where(last_row > 0, c["rows_in"][1].astype(F32), 0.0).astype(BF)
    for k in range(3):
        row_ok = (first_row, 1.0, last_row)[k]
        left = c["cols_in"][3 + (1, 0, -1)[k] + 1].astype(F32)[0:72].reshape(9, 8, 128)
        right = c["cols_in"][(1, 0, -1)[k] + 1].astype(F32)[0:72].reshape(9, 8, 128)
        left = jnp.where(row_ok * first_col > 0, left, 0.0)
        right = jnp.where(row_ok * last_col > 0, right, 0.0)
        for g in range(4):
            to_left = pltpu.roll(left, (128 - 32 * g) % 128, 2) if g else left
            to_right = pltpu.roll(right, (160 - 32 * g) % 128, 2) if g != 1 else right
            piece = jnp.where(lane9 < 32, to_left, jnp.where(lane9 < 64, to_right, 0.0))
            c["ext_side"][:, 32 * k + 8 * g : 32 * k + 8 * g + 8, :] = piece
    c["ext"][:, :, 256:384] = c["ext_side"][...].astype(BF)

    def spread_channel(ch, _):
        wide = jnp.dot(c["ext"][ch], c["spread"][...], preferred_element_type=F32)
        for k in range(4):
            c["planar"][k, pl.ds(pl.multiple_of(ch * 96, 96), 96), :] = wide[:, 128 * k : 128 * k + 128]
        return 0

    lax.fori_loop(0, 9, spread_channel, 0, unroll=9)

    def gather_row(y, _):
        for k in range(4):
            c["rows_yc"][y, :, 128 * k : 128 * k + 128] = c["planar"][k, pl.ds(y + 12, 16, stride=96), :].astype(BF)
        return 0

    lax.fori_loop(0, 72, gather_row, 0, unroll=24)

    def column_cap(number, first, count, origin, width):
        np_ = NP[number]
        n = 4 * np_
        at = origin + 2 * (first + iota((count, n), 0)) + (iota((count, n), 1) // np_) % 2 + tx * width
        return jnp.where((at >= 0) & (at < width * cols_tx), BIG, 0.0)

    def edges(wp, origin, width):
        low = (-(origin // 2) + 7) // 8 * 8
        return low, min((width - origin) // 2 // 8 * 8, wp)

    def finish(number, r, caps, i0, g, wp, origin_y, origin_x, height, width):
        np_ = NP[number]
        n = 4 * np_
        u = jnp.maximum(r + table[number : number + 1, 0:n], 0.0)
        low, high = edges(wp, origin_x, width)
        pieces = []
        for k in range(g):
            v = u[k * wp : (k + 1) * wp]
            parts = [jnp.minimum(v[0:low], caps[0])] if low else []
            parts = parts + ([v[low:high]] if high > low else [])
            parts = parts + ([jnp.minimum(v[high:wp], caps[1])] if wp > high else [])
            v = jnp.concatenate(parts, axis=0) if len(parts) > 1 else parts[0]
            y = origin_y + 2 * (i0 + k)
            if y < 0 or y + 2 > height:
                at = y + iota((1, n), 1) // (2 * np_) + ty * height
                v = jnp.minimum(v, jnp.where((at >= 0) & (at < height * rows_ty), BIG, 0.0))
            pieces.append(v)
        return pieces

    def to_blocks(pieces, target, i0, wp, n):
        t = c["t%d" % n]
        g = len(pieces)
        if target.shape[2] == n:
            for k in range(g):
                target[i0 + k, :, :] = pieces[k].astype(BF)
            return
        for k in range(g):
            t[k * wp : (k + 1) * wp, :] = pieces[k]
            target[i0 + k, :, 0:n] = pieces[k].astype(BF)
        for k in range(g):
            target[i0 + k, :, n : 2 * n] = t[k * wp + 1 : (k + 1) * wp + 1, :].astype(BF)

    def pooled(piece, np_):
        if np_ == 32:
            m = jnp.maximum(piece, pltpu.roll(piece, 64, 1))
            return jnp.maximum(m, pltpu.roll(m, 32, 1))
        if np_ == 64:
            m = jnp.maximum(piece[:, 0:128], piece[:, 128:256])
            return jnp.maximum(m, pltpu.roll(m, 64, 1))
        m = jnp.maximum(piece[:, 0:128], piece[:, 128:256])
        return jnp.maximum(m, jnp.maximum(piece[:, 256:384], piece[:, 384:512]))

    def pack(pixels, target, first, count, wp, lanes, row0, col0):
        lane = iota((wp, 128), 1)

        def step(i, _):
            a = [
                [pixels[row0 + 2 * i + py, pl.ds(col0 + m, wp, stride=2), :] for m in range(4)] for py in range(2)
            ]
            for u in range(2):
                four = [a[0][2 * u], a[0][2 * u + 1], a[1][2 * u], a[1][2 * u + 1]]
                base = u * 4 * lanes
                if lanes == 32:
                    v = jnp.where(
                        lane < 64,
                        jnp.where(lane < 32, four[0], four[1]),
                        jnp.where(lane < 96, four[2], four[3]),
                    )
                    target[i, :, base : base + 128] = v.astype(BF)
                elif lanes == 64:
                    for py in range(2):
                        v = jnp.where(lane < 64, four[2 * py], four[2 * py + 1])
                        target[i, :, base + 128 * py : base + 128 * py + 128] = v.astype(BF)
                else:
                    for q in range(4):
                        target[i, :, base + 128 * q : base + 128 * q + 128] = four[q].astype(BF)
            return 0

        lax.fori_loop(first, first + count, step, 0, unroll=True)

    def to_pixels(pieces, target, i0, wp, wr, np_):
        td = c["td"]
        lane = iota((wp, 128), 1)
        lane_r = iota((wr, 128), 1)
        for k in range(len(pieces)):
            for qy in range(2):
                at = 2 * k + qy
                if np_ == 128:
                    even = pieces[k][:, 256 * qy : 256 * qy + 128]
                    odd = pieces[k][:, 256 * qy + 128 : 256 * qy + 256]
                else:
                    v = pieces[k][:, 128 * qy : 128 * qy + 128]
                    w = pltpu.roll(v, 64, 1)
                    even = jnp.where(lane < 64, v, w)
                    odd = jnp.where(lane < 64, w, v)
                td[at, pl.ds(0, wp, stride=2), :] = even
                td[at, pl.ds(1, wp, stride=2), :] = odd
        for k in range(len(pieces)):
            for qy in range(2):
                at = 2 * k + qy
                here, right = td[at, 0:wr, :], td[at, 1 : wr + 1, :]
                if np_ == 128:
                    target[2 * (i0 + k) + qy, :, 0:128] = here.astype(BF)
                    target[2 * (i0 + k) + qy, :, 128:256] = right.astype(BF)
                else:
                    target[2 * (i0 + k) + qy, :, :] = jnp.where(lane_r < 64, here, right).astype(BF)

    def block_input(ref):
        def load(i0, g):
            lanes = ref.shape[2]
            rows = g * ref.shape[1]
            return [
                ref[pl.ds(i0, g)].reshape(rows, lanes),
                ref[pl.ds(i0 + 1, g)].reshape(rows, lanes),
            ]

        return load

    def layer(number, loads, first, count, g, wp, origin_y, origin_x, level, store):
        height, width = 32 >> level, 256 >> level
        low, high = edges(wp, origin_x, width)
        caps = (
            column_cap(number, 0, low, origin_x, width) if low else None,
            column_cap(number, high, wp - high, origin_x, width) if wp > high else None,
        )

        def step(it, _):
            i0 = first + it * g
            lhs = []
            for load in loads:
                lhs = lhs + load(i0, g)
            lhs = jnp.concatenate(lhs, axis=1) if len(lhs) > 1 else lhs[0]
            if number in FLIPPED:
                r = jnp.dot(lhs, c["w%d" % number][...], preferred_element_type=F32)
            else:
                r = nt(lhs, c["w%d" % number][...])
            if number in SPLIT:
                c["t128"][0 : g * wp, :] = r[:, 128:256]
                r = r[:, 0:128] + c["t128"][1 : g * wp + 1, :]
            store(finish(number, r, caps, i0, g, wp, origin_y, origin_x, height, width), i0)
            return 0

        for it in range(count):
            step(it, 0)

    def pool_into(pixels, number, wp):
        def store(pieces, i0):
            for k, piece in enumerate(pieces):
                pixels[i0 + k, 0:wp, :] = pooled(piece, NP[number])

        return store

    def windows(first, count, g):
        t = c["t128"]

        def step(it, _):
            i0 = first + it * g
            for k in range(g):
                rows = c["rows_yc"][pl.ds(2 * (i0 + k), 4)].reshape(64, 512)
                stacked = jnp.concatenate([rows[:, 0:256], rows[:, 256:512]], axis=0)
                turned = nt(c["eye"][...], stacked)
                c["fwin"][i0 + k, :, 0:128] = turned.astype(BF)
                t[k * 160 : (k + 1) * 160, :] = turned
            for k in range(g):
                c["fwin"][i0 + k, :, 128:256] = t[k * 160 + 1 : (k + 1) * 160 + 1, :].astype(BF)
            return 0

        for it in range(count):
            step(it, 0)

    def window_load(i0, g):
        return [c["fwin"][pl.ds(i0, g)].reshape(g * 160, 256)]

    def conv0(first, count, g):
        layer(0, [window_load], first, count, g, 160, -19, -35, 0, lambda p, i0: to_blocks(p, c["s1"], i0, 160, 128))

    def conv1(first, count, g):
        layer(1, [block_input(c["s1"])], first, count, g, 160, -18, -34, 0, pool_into(c["pix1"], 1, 160))

    def conv2(first, count, g):
        layer(2, [block_input(c["s2"])], first, count, g, 80, -8, -8, 1, pool_into(c["pix2"], 2, 80))

    windows(6, 2, 12)
    conv0(6, 2, 12)
    conv1(6, 2, 11)
    pack(c["pix1"], c["s2"], 3, 11, 80, 32, 0, 8)
    conv2(3, 1, 10)
    pack(c["pix2"], c["s3"], 0, 5, 48, 64, 3, 3)
    layer(3, [block_input(c["s3"])], 0, 1, 4, 48, 0, 0, 2, pool_into(c["pix3o"], 3, 48))

    lane8 = iota((8, 128), 1)
    pieces = []
    for half in range(2):
        for y in range(4):
            even = c["pix3o"][y, pl.ds(16 * half, 8, stride=2), :]
            odd = c["pix3o"][y, pl.ds(16 * half + 1, 8, stride=2), :]
            pieces.append(jnp.where(lane8 < 64, even, odd))
    c["tile_out"][...] = jnp.concatenate(pieces, axis=0).astype(BF)
    copies = []
    for number, (dy, dx) in enumerate(FAR):
        rows = pl.ds(0, 64) if dx == 0 else pl.ds(32, 32) if dx == 1 else pl.ds(0, 32)
        copy = pltpu.make_async_remote_copy(
            src_ref=c["tile_out"].at[rows],
            dst_ref=c["tiles_in"].at[number, rows],
            send_sem=send2.at[number],
            recv_sem=recv2.at[number],
            device_id=device(dy, dx),
            device_id_type=MESH,
        )
        copies.append((dy, dx, copy))

    wait = exchange(copies)

    windows(0, 1, 6)
    windows(30, 1, 5)
    conv0(0, 1, 6)
    conv0(30, 1, 5)
    conv1(0, 1, 6)
    conv1(28, 1, 6)
    pack(c["pix1"], c["s2"], 0, 3, 80, 32, 0, 8)
    pack(c["pix1"], c["s2"], 14, 3, 80, 32, 0, 8)
    conv2(0, 1, 3)
    conv2(13, 1, 3)
    pack(c["pix1"], c["k11"], 0, 12, 80, 32, 5, 13)
    pack(c["pix2"], c["k9"], 0, 8, 48, 64, 0, 0)

    wait()

    slot = {d: n for n, d in enumerate(FAR)}
    for ky in range(-3, 4):
        for kx in range(-1, 2):
            if (ky, kx) == (0, 0):
                tile = c["tile_out"][...].astype(F32)
            else:
                ok = (ty + ky >= 0) & (ty + ky < rows_ty) & (tx + kx >= 0) & (tx + kx < cols_tx)
                tile = jnp.where(jnp.where(ok, 1.0, 0.0) > 0, c["tiles_in"][slot[-ky, -kx]].astype(F32), 0.0)
            halves = (0, 1) if kx == 0 else (1,) if kx == -1 else (0,)
            for y in range(4):
                if ky == -3 and y < 3 or ky == 3 and y > 0:
                    continue
                for half in halves:
                    v = tile[32 * half + 8 * y : 32 * half + 8 * y + 8]
                    w = pltpu.roll(v, 64, 1)
                    row = 12 + 4 * ky + y
                    col = 32 * (kx + 1) + 16 * half
                    c["pix3"][row, pl.ds(col, 8, stride=2), :] = jnp.where(lane8 < 64, v, w)
                    c["pix3"][row, pl.ds(col + 1, 8, stride=2), :] = jnp.where(lane8 < 64, w, v)

    pack(c["pix3"], c["s4"], 0, 11, 32, 64, 3, 23)
    pack(c["pix3"], c["k7"], 0, 6, 32, 64, 8, 28)

    layer(4, [block_input(c["s4"])], 0, 1, 10, 32, -8, -8, 3, pool_into(c["pix4"], 4, 32))
    pack(c["pix4"], c["s5"], 0, 5, 16, 128, 0, 0)
    layer(5, [block_input(c["s5"])], 0, 1, 4, 16, -3, -3, 4, lambda p, i0: to_blocks(p, c["s6"], i0, 16, 512))
    layer(6, [block_input(c["s6"])], 0, 1, 3, 16, -2, -2, 4, lambda p, i0: to_pixels(p, c["r7"], i0, 16, 32, 128))
    layer(
        7, [block_input(c["r7"]), block_input(c["k7"])], 0, 1, 5, 32, -3, -3, 3,
        lambda p, i0: to_blocks(p, c["s8"], i0, 32, 512),
    )
    layer(8, [block_input(c["s8"])], 0, 1, 4, 32, -2, -2, 3, lambda p, i0: to_pixels(p, c["r9"], i0, 32, 48, 128))
    layer(
        9, [block_input(c["r9"]), block_input(c["k9"])], 0, 1, 7, 48, -3, -3, 2,
        lambda p, i0: to_blocks(p, c["s10"], i0, 48, 512),
    )
    layer(10, [block_input(c["s10"])], 0, 1, 6, 48, -2, -2, 2, lambda p, i0: to_pixels(p, c["r11"], i0, 48, 80, 128))
    layer(
        11, [block_input(c["r11"]), block_input(c["k11"])], 0, 1, 11, 80, -3, -3, 1,
        lambda p, i0: to_blocks(p, c["s12"], i0, 80, 256),
    )
    layer(12, [block_input(c["s12"])], 0, 1, 10, 80, -2, -2, 1, lambda p, i0: to_pixels(p, c["r13"], i0, 80, 144, 64))

    def features_load(i0, g):
        return [c["fwin"][pl.ds(i0 + 8, g), 16:160, :].reshape(g * 144, 256)]

    layer(
        13, [block_input(c["r13"]), features_load], 0, 1, 10, 144, -3, -3, 0,
        lambda p, i0: to_blocks(p, c["s14"], i0, 144, 256),
    )
    layer(
        13, [block_input(c["r13"]), features_load], 10, 1, 9, 144, -3, -3, 0,
        lambda p, i0: to_blocks(p, c["s14"], i0, 144, 256),
    )
    layer(14, [block_input(c["s14"])], 0, 2, 9, 144, -2, -2, 0, lambda p, i0: to_blocks(p, c["s15"], i0, 144, 128))

    lane144 = iota((16, 144), 1)

    def last(i, _):
        field = jnp.concatenate([c["s15"][i], c["s15"][i + 1]], axis=1)
        r = nt(c["w15"][...], field)
        r = r[0:16] + pltpu.roll(r[16:32], 143, 1) + c["column"][...]
        r = jnp.where(lane144 < 129, r, 0.0)
        c["z0"][pl.ds(pl.multiple_of(8 * i, 8), 8), :] = r[0:8]
        c["z1"][pl.ds(pl.multiple_of(8 * i, 8), 8), :] = r[8:16]
        return 0

    c["z0"][136:144, :] = jnp.zeros((8, 144), F32)
    c["z1"][136:144, :] = jnp.zeros((8, 144), F32)
    lax.fori_loop(0, 17, last, 0, unroll=17)
    at = iota((144, 256), 1) - 2 * iota((144, 256), 0)
    even = (at == -1).astype(F32).astype(BF)
    odd = (at == 0).astype(F32).astype(BF)
    wide = jnp.dot(c["z0"][...].astype(BF), even, preferred_element_type=F32) + jnp.dot(
        c["z1"][...].astype(BF), odd, preferred_element_type=F32
    )
    for half in range(2):
        lanes = slice(128 * half, 128 * half + 128)
        c["zf"][half] = wide[:, lanes]
        for o in range(3):
            c["out32"][2 * o + half, pl.ds(0, 16, stride=2), :] = c["zf"][half, pl.ds(3 + o, 16, stride=8), :]
            c["out32"][2 * o + half, pl.ds(1, 16, stride=2), :] = c["zf"][half, pl.ds(8 + o, 16, stride=8), :]
            out[o, :, lanes] = c["out32"][2 * o + half].astype(BF)


def body(sizes, features, *rest):
    weights, biases = list(rest[:16]), rest[16]
    for number in FLIPPED:
        weights[number] = jnp.transpose(weights[number], (0, 1, 3, 2) if number else (0, 3, 1, 2))
    vmem = pl.BlockSpec(memory_space=pltpu.VMEM)
    scratch = [pltpu.VMEM(shape, kind) for shape, kind in SCRATCH.values()]
    scratch += [pltpu.SemaphoreType.DMA((n,)) for n in (8, 8, 20, 20)]
    scratch += [pltpu.VMEM(w.shape, BF) for w in weights] + [pltpu.SemaphoreType.DMA((16,))]
    return pl.pallas_call(
        functools.partial(kernel, sizes),
        out_shape=jax.ShapeDtypeStruct((3, 32, 256), BF),
        in_specs=[vmem] + [pl.BlockSpec(memory_space=pl.ANY)] * 16 + [vmem],
        out_specs=vmem,
        scratch_shapes=scratch,
        compiler_params=pltpu.CompilerParams(
            collective_id=0, has_side_effects=True, vmem_limit_bytes=58 << 20
        ),
    )(features, *weights, biases)


def solution(mesh):
    sizes = (mesh.shape["ty"], mesh.shape["tx"])
    return jax.shard_map(
        functools.partial(body, sizes),
        mesh=mesh,
        in_specs=(P(None, "ty", "tx"),) + (P(),) * 17,
        out_specs=P(None, "ty", "tx"),
        check_vma=False,
    )
```

```python
import functools

import jax
import jax.numpy as jnp
from jax import lax
from jax.experimental import pallas as pl
from jax.experimental.pallas import tpu as pltpu
from jax.sharding import PartitionSpec as P

F32 = jnp.float32
BF = jnp.bfloat16
BIG = 3.0e38
MESH = pl.DeviceIdType.MESH

COUT = [32, 32, 48, 64, 80, 96, 96, 112, 112, 96, 96, 64, 64, 64, 32, 3]
CIN = [9, 32, 32, 48, 64, 80, 96, 160, 112, 160, 96, 128, 64, 73, 64, 32]
NP = [32, 32, 64, 64, 128, 128, 128, 128, 128, 128, 128, 64, 64, 64, 32, 4]
KDIM = [256, 256, 512, 1024, 1024, 2048, 2048, 1536, 2048, 1536, 2048, 1024, 1024, 512, 512, 256]
SPLIT = (1, 14, 15)
DIRS = [(dy, dx) for dy in (-1, 0, 1) for dx in (-1, 0, 1) if (dy, dx) != (0, 0)]
FAR = DIRS + [(dy, dx) for dy in (-3, -2, 2, 3) for dx in (-1, 0, 1)]

SCRATCH = dict(
    rows_in=((2, 9, 32, 256), BF),
    cols_out=((2, 80, 128), BF),
    cols_in=((6, 80, 128), BF),
    tile_out=((64, 128), BF),
    tiles_in=((20, 64, 128), BF),
    ext_side=((9, 96, 128), F32),
    ext=((9, 96, 384), BF),
    spread=((384, 512), BF),
    planar=((4, 16 * 96, 128), F32),
    rows_yc=((72, 16, 512), BF),
    eye=((160, 256), BF),
    fwin=((40, 160, 256), BF),
    s1=((36, 160, 128), BF),
    pix1=((34, 176, 128), F32),
    s2=((17, 80, 256), BF),
    pix2=((16, 112, 128), F32),
    s3=((5, 48, 512), BF),
    pix3o=((4, 48, 128), F32),
    pix3=((28, 112, 128), F32),
    s4=((11, 32, 512), BF),
    pix4=((10, 48, 128), F32),
    s5=((5, 16, 1024), BF),
    s6=((4, 16, 1024), BF),
    r7=((6, 32, 256), BF),
    k7=((6, 32, 512), BF),
    s8=((5, 32, 1024), BF),
    r9=((8, 48, 256), BF),
    k9=((8, 48, 512), BF),
    s10=((7, 48, 1024), BF),
    r11=((12, 80, 256), BF),
    k11=((12, 80, 256), BF),
    s12=((11, 80, 512), BF),
    r13=((24, 144, 128), BF),
    s14=((21, 144, 256), BF),
    s15=((20, 144, 128), BF),
    t128=((1928, 128), F32),
    t256=((1448, 256), F32),
    t512=((360, 512), F32),
    td=((20, 184, 128), F32),
    w15f=((32, 256), F32),
    flat=((16, 128), F32),
    table=((16, 512), F32),
    column=((16, 144), F32),
    z0=((144, 144), F32),
    z1=((144, 144), F32),
    zf=((2, 144, 128), F32),
    out32=((6, 32, 128), F32),
)
for _k in range(16):
    _n = 32 if _k == 15 else 256 if _k in SPLIT else 4 * NP[_k]
    SCRATCH["w%d" % _k] = ((KDIM[_k], _n) if _k in (0, 2, 3, 4, 5, 7, 9) else (_n, KDIM[_k]), BF)


def iota(shape, dim):
    return lax.broadcasted_iota(jnp.int32, shape, dim)


def nt(a, b):
    return lax.dot_general(a, b, (((1,), (1,)), ((), ())), preferred_element_type=F32)


FLIPPED = (0, 2, 3, 4, 5, 7, 9)


def tap_of(w, number, ky, kx, first, count):
    if number == 0:
        return w[ky, :, kx, :]
    if number in FLIPPED:
        return w[ky, kx, first : first + count, :]
    return w[ky, kx][:, first : first + count]


def put(wt, number, n, k, tap):
    if number in FLIPPED:
        wt[k : k + tap.shape[0], n : n + tap.shape[1]] = tap
    else:
        wt[n : n + tap.shape[0], k : k + tap.shape[1]] = tap


def prepare_blocks(wt, w, number, offset, first, count, lanes):
    for ky in range(3):
        for kx in range(3):
            tap = tap_of(w, number, ky, kx, first, count)
            for qy in range(2):
                for qx in range(2):
                    r, s = ky + qy, kx + qx
                    n = (qy * 2 + qx) * NP[number]
                    if number in SPLIT:
                        k = (r // 2 * 4 + r % 2 * 2 + s % 2) * lanes
                        n = n + s // 2 * 128
                    else:
                        k = offset + ((r // 2 * 2 + s // 2) * 4 + r % 2 * 2 + s % 2) * lanes
                    put(wt, number, n, k, tap)


def prepare_window(wt, w, number, offset, first):
    for ky in range(3):
        for kx in range(3):
            tap = tap_of(w, number, ky, kx, first, 9)
            for qy in range(2):
                for qx in range(2):
                    k = offset + (kx + qx) * 64 + (ky + qy) * 16
                    put(wt, number, (qy * 2 + qx) * NP[number], k, tap)


SUMS = {(0, 0): (0, 1), (0, 1): (2,), (1, 0): (0,), (1, 1): (1, 2)}


def prepare_up(wt, w, number, count, lanes):
    taps = [[tap_of(w, number, ky, kx, 0, count).astype(F32) for kx in range(3)] for ky in range(3)]
    for qy in range(2):
        for t in range(2):
            rows = SUMS[qy, t]
            line = taps[rows[0]] if len(rows) == 1 else [taps[rows[0]][kx] + taps[rows[1]][kx] for kx in range(3)]
            for qx in range(2):
                for u in range(2):
                    cols = SUMS[qx, u]
                    total = line[cols[0]] if len(cols) == 1 else line[cols[0]] + line[cols[1]]
                    put(wt, number, (qy * 2 + qx) * NP[number], (t * 2 + u) * lanes, total.astype(BF))


def prepare_biases(biases, flat, table, column):
    flat[...] = jnp.zeros(flat.shape, F32)
    for r in range(8):
        flat[r : r + 1, :] = biases[pl.ds(128 * r, 128)].reshape(1, 128)
    flat[8:9, 0:67] = biases[pl.ds(1024, 67)].reshape(1, 67)
    lane = iota((8, 128), 1)
    offset = 0
    for number in range(16):
        r, m = offset // 128, offset % 128
        offset = offset + COUT[number]
        pair = jnp.concatenate([flat[r : r + 1, :], flat[r + 1 : r + 2, :]], axis=1)
        pair = jnp.broadcast_to(pair, (8, 256))
        if m:
            pair = pltpu.roll(pair, 256 - m, 1)
        value = jnp.where(lane < COUT[number], pair[:, 0:128], 0.0)
        if number == 15:
            row = iota((16, 128), 0) % 8
            twice = jnp.concatenate([value, value], axis=0)
            mine = jnp.where((iota((16, 128), 1) == row % 3) & (row < 6), twice, 0.0)
            column[...] = jnp.broadcast_to(jnp.sum(mine, axis=1, keepdims=True), (16, 144))
            continue
        if NP[number] == 32:
            value = value + pltpu.roll(value, 32, 1)
        if NP[number] <= 64:
            value = value + pltpu.roll(value, 64, 1)
        for k in range(4 * NP[number] // 128):
            table[number : number + 1, 128 * k : 128 * k + 128] = value[0:1]


def kernel(sizes, feat, *refs):
    rows_ty, cols_tx = sizes
    sources = refs[:16]
    weights = refs[-17:-1]
    weight_sem = refs[-1]
    loads = [pltpu.make_async_copy(sources[k], weights[k], weight_sem.at[k]) for k in range(16)]
    out = refs[17]
    c = dict(zip(SCRATCH, refs[18 : 18 + len(SCRATCH)]))
    send1, recv1, send2, recv2 = refs[18 + len(SCRATCH) : 22 + len(SCRATCH)]
    table = c["table"]
    ty = lax.axis_index("ty")
    tx = lax.axis_index("tx")

    def device(dy, dx):
        return (ty + dy, tx + dx)

    def exists(dy, dx):
        found = None
        for here, step, size in ((ty, dy, rows_ty), (tx, dx, cols_tx)):
            if step:
                inside = here + step < size if step > 0 else here + step >= 0
                found = inside if found is None else found & inside
        return found

    def exchange(copies):
        for dy, dx, copy in sorted(copies, key=lambda c: c[1] == 0):
            pl.when(exists(dy, dx))(copy.start)

        def wait():
            for dy, dx, copy in copies:
                pl.when(exists(dy, dx))(copy.wait_send)
                pl.when(exists(-dy, -dx))(copy.wait_recv)

        return wait

    barrier = pltpu.get_barrier_semaphore()
    for dy, dx in sorted(FAR, key=lambda d: d[1] == 0):

        @pl.when(exists(dy, dx))
        def greet(dy=dy, dx=dx):
            pl.semaphore_signal(barrier, inc=1, device_id=device(dy, dx), device_id_type=MESH)


    for load in loads:
        load.start()

    lane9 = iota((9, 8, 128), 2)
    for side in range(2):
        value = jnp.zeros((9, 8, 128), F32)
        for g in range(4):
            piece = feat[:, 8 * g : 8 * g + 8, 128 * side : 128 * side + 128].astype(F32)
            shift = (32 * g - 96 * side) % 128
            if shift:
                piece = pltpu.roll(piece, shift, 2)
            value = jnp.where((lane9 >= 32 * g) & (lane9 < 32 * g + 32), piece, value)
        c["cols_out"][side, 0:72, :] = value.reshape(72, 128).astype(BF)
        c["cols_out"][side, 64:80, :] = jnp.concatenate(
            [value.reshape(72, 128)[64:72], jnp.zeros((8, 128), F32)], 0
        ).astype(BF)

    def clear(number):
        c["w%d" % number][...] = jnp.zeros(c["w%d" % number].shape, BF)

    for number in range(4):
        clear(number)
    for load in loads[:4]:
        load.wait()
    prepare_window(c["w0"], weights[0], 0, 0, 0)
    prepare_blocks(c["w1"], weights[1], 1, 0, 0, 32, 32)
    prepare_blocks(c["w2"], weights[2], 2, 0, 0, 32, 32)
    prepare_blocks(c["w3"], weights[3], 3, 0, 0, 48, 64)
    prepare_biases(refs[16], c["flat"], c["table"], c["column"])

    place = iota((384, 128), 0)
    x = jnp.where(place < 256, place, jnp.where(place < 288, place - 288, jnp.where(place < 320, place - 32, -1000)))
    x = x - 2 * iota((384, 128), 1) + 36
    for px in range(2):
        for half in range(2):
            hit = jnp.where(x == px + 256 * half, 1.0, 0.0)
            c["spread"][:, 256 * px + 128 * half : 256 * px + 128 * half + 128] = hit.astype(BF)
    c["eye"][...] = (iota((160, 256), 0) == iota((160, 256), 1)).astype(F32).astype(BF)
    for k in range(4):
        c["planar"][k, 864:1536, :] = jnp.zeros((672, 128), F32)

    def reach(here, size, most):
        total = 1
        for k in range(1, most + 1):
            total = total + lax.div(here + size - k, size) + 1 - lax.div(here + k, size)
        return total

    pl.semaphore_wait(barrier, reach(ty, rows_ty, 3) * reach(tx, cols_tx, 1) - 1)
    copies = []
    for number, (dy, dx) in enumerate(DIRS):
        if dx == 0:
            source, target = feat, c["rows_in"].at[0 if dy == 1 else 1]
        else:
            source = c["cols_out"].at[0 if dx == -1 else 1]
            target = c["cols_in"].at[(0 if dx == -1 else 3) + dy + 1]
        copy = pltpu.make_async_remote_copy(
            src_ref=source,
            dst_ref=target,
            send_sem=send1.at[number],
            recv_sem=recv1.at[number],
            device_id=device(dy, dx),
            device_id_type=MESH,
        )
        copies.append((dy, dx, copy))

    wait = exchange(copies)

    for number in range(4, 15):
        clear(number)
    for load in loads[4:]:
        load.wait()
    prepare_blocks(c["w4"], weights[4], 4, 0, 0, 64, 64)
    prepare_blocks(c["w5"], weights[5], 5, 0, 0, 80, 128)
    prepare_blocks(c["w6"], weights[6], 6, 0, 0, 96, 128)
    prepare_up(c["w7"], weights[7], 7, 96, 128)
    prepare_blocks(c["w7"], weights[7], 7, 512, 96, 64, 64)
    prepare_blocks(c["w8"], weights[8], 8, 0, 0, 112, 128)
    prepare_up(c["w9"], weights[9], 9, 112, 128)
    prepare_blocks(c["w9"], weights[9], 9, 512, 112, 48, 64)
    prepare_blocks(c["w10"], weights[10], 10, 0, 0, 96, 128)
    prepare_up(c["w11"], weights[11], 11, 96, 128)
    prepare_blocks(c["w11"], weights[11], 11, 512, 96, 32, 32)
    prepare_blocks(c["w12"], weights[12], 12, 0, 0, 64, 64)
    prepare_up(c["w13"], weights[13], 13, 64, 64)
    prepare_window(c["w13"], weights[13], 13, 256, 64)
    prepare_blocks(c["w14"], weights[14], 14, 0, 0, 64, 64)
    c["w15f"][...] = jnp.zeros((32, 256), F32)
    for ky in range(3):
        for kx in range(3):
            tap = weights[15][ky, kx].astype(F32)
            for qy in range(2):
                for qx in range(2):
                    r, s = ky + qy, kx + qx
                    k = (r // 2 * 4 + r % 2 * 2 + s % 2) * 32
                    n = s // 2 * 16 + qx * 8 + qy * 3
                    c["w15f"][n : n + 3, k : k + 32] = tap
    c["w15"][...] = c["w15f"][...].astype(BF)
    wait()

    first_row = jnp.where(ty > 0, 1.0, 0.0)
    last_row = jnp.where(ty < rows_ty - 1, 1.0, 0.0)
    first_col = jnp.where(tx > 0, 1.0, 0.0)
    last_col = jnp.where(tx < cols_tx - 1, 1.0, 0.0)
    c["ext"][:, 0:32, 0:256] = jnp.where(first_row > 0, c["rows_in"][0].astype(F32), 0.0).astype(BF)
    c["ext"][:, 32:64, 0:256] = feat[...]
    c["ext"][:, 64:96, 0:256] = jnp.where(last_row > 0, c["rows_in"][1].astype(F32), 0.0).astype(BF)
    for k in range(3):
        row_ok = (first_row, 1.0, last_row)[k]
        left = c["cols_in"][3 + (1, 0, -1)[k] + 1].astype(F32)[0:72].reshape(9, 8, 128)
        right = c["cols_in"][(1, 0, -1)[k] + 1].astype(F32)[0:72].reshape(9, 8, 128)
        left = jnp.where(row_ok * first_col > 0, left, 0.0)
        right = jnp.where(row_ok * last_col > 0, right, 0.0)
        for g in range(4):
            to_left = pltpu.roll(left, (128 - 32 * g) % 128, 2) if g else left
            to_right = pltpu.roll(right, (160 - 32 * g) % 128, 2) if g != 1 else right
            piece = jnp.where(lane9 < 32, to_left, jnp.where(lane9 < 64, to_right, 0.0))
            c["ext_side"][:, 32 * k + 8 * g : 32 * k + 8 * g + 8, :] = piece
    c["ext"][:, :, 256:384] = c["ext_side"][...].astype(BF)

    def spread_channel(ch, _):
        wide = jnp.dot(c["ext"][ch], c["spread"][...], preferred_element_type=F32)
        for k in range(4):
            c["planar"][k, pl.ds(pl.multiple_of(ch * 96, 96), 96), :] = wide[:, 128 * k : 128 * k + 128]
        return 0

    lax.fori_loop(0, 9, spread_channel, 0, unroll=9)

    def gather_row(y, _):
        for k in range(4):
            c["rows_yc"][y, :, 128 * k : 128 * k + 128] = c["planar"][k, pl.ds(y + 12, 16, stride=96), :].astype(BF)
        return 0

    lax.fori_loop(0, 72, gather_row, 0, unroll=72)

    def column_cap(number, first, count, origin, width):
        np_ = NP[number]
        n = 4 * np_
        at = origin + 2 * (first + iota((count, n), 0)) + (iota((count, n), 1) // np_) % 2 + tx * width
        return jnp.where((at >= 0) & (at < width * cols_tx), BIG, 0.0)

    def edges(wp, origin, width):
        low = (-(origin // 2) + 7) // 8 * 8
        return low, min((width - origin) // 2 // 8 * 8, wp)

    def finish(number, r, caps, i0, g, wp, origin_y, origin_x, height, width):
        np_ = NP[number]
        n = 4 * np_
        u = jnp.maximum(r + table[number : number + 1, 0:n], 0.0)
        low, high = edges(wp, origin_x, width)
        pieces = []
        for k in range(g):
            v = u[k * wp : (k + 1) * wp]
            parts = [jnp.minimum(v[0:low], caps[0])] if low else []
            parts = parts + ([v[low:high]] if high > low else [])
            parts = parts + ([jnp.minimum(v[high:wp], caps[1])] if wp > high else [])
            v = jnp.concatenate(parts, axis=0) if len(parts) > 1 else parts[0]
            y = origin_y + 2 * (i0 + k)
            if y < 0 or y + 2 > height:
                at = y + iota((1, n), 1) // (2 * np_) + ty * height
                v = jnp.minimum(v, jnp.where((at >= 0) & (at < height * rows_ty), BIG, 0.0))
            pieces.append(v)
        return pieces

    def to_blocks(pieces, target, i0, wp, n):
        t = c["t%d" % n]
        g = len(pieces)
        if target.shape[2] == n:
            for k in range(g):
                target[i0 + k, :, :] = pieces[k].astype(BF)
            return
        for k in range(g):
            t[k * wp : (k + 1) * wp, :] = pieces[k]
            target[i0 + k, :, 0:n] = pieces[k].astype(BF)
        for k in range(g):
            target[i0 + k, :, n : 2 * n] = t[k * wp + 1 : (k + 1) * wp + 1, :].astype(BF)

    def pooled(piece, np_):
        if np_ == 32:
            m = jnp.maximum(piece, pltpu.roll(piece, 64, 1))
            return jnp.maximum(m, pltpu.roll(m, 32, 1))
        if np_ == 64:
            m = jnp.maximum(piece[:, 0:128], piece[:, 128:256])
            return jnp.maximum(m, pltpu.roll(m, 64, 1))
        m = jnp.maximum(piece[:, 0:128], piece[:, 128:256])
        return jnp.maximum(m, jnp.maximum(piece[:, 256:384], piece[:, 384:512]))

    def pack(pixels, target, first, count, wp, lanes, row0, col0):
        lane = iota((wp, 128), 1)

        def step(i, _):
            a = [
                [pixels[row0 + 2 * i + py, pl.ds(col0 + m, wp, stride=2), :] for m in range(4)] for py in range(2)
            ]
            for u in range(2):
                four = [a[0][2 * u], a[0][2 * u + 1], a[1][2 * u], a[1][2 * u + 1]]
                base = u * 4 * lanes
                if lanes == 32:
                    v = jnp.where(
                        lane < 64,
                        jnp.where(lane < 32, four[0], four[1]),
                        jnp.where(lane < 96, four[2], four[3]),
                    )
                    target[i, :, base : base + 128] = v.astype(BF)
                elif lanes == 64:
                    for py in range(2):
                        v = jnp.where(lane < 64, four[2 * py], four[2 * py + 1])
                        target[i, :, base + 128 * py : base + 128 * py + 128] = v.astype(BF)
                else:
                    for q in range(4):
                        target[i, :, base + 128 * q : base + 128 * q + 128] = four[q].astype(BF)
            return 0

        lax.fori_loop(first, first + count, step, 0, unroll=True)

    def to_pixels(pieces, target, i0, wp, wr, np_):
        td = c["td"]
        lane = iota((wp, 128), 1)
        lane_r = iota((wr, 128), 1)
        for k in range(len(pieces)):
            for qy in range(2):
                at = 2 * k + qy
                if np_ == 128:
                    even = pieces[k][:, 256 * qy : 256 * qy + 128]
                    odd = pieces[k][:, 256 * qy + 128 : 256 * qy + 256]
                else:
                    v = pieces[k][:, 128 * qy : 128 * qy + 128]
                    w = pltpu.roll(v, 64, 1)
                    even = jnp.where(lane < 64, v, w)
                    odd = jnp.where(lane < 64, w, v)
                td[at, pl.ds(0, wp, stride=2), :] = even
                td[at, pl.ds(1, wp, stride=2), :] = odd
        for k in range(len(pieces)):
            for qy in range(2):
                at = 2 * k + qy
                here, right = td[at, 0:wr, :], td[at, 1 : wr + 1, :]
                if np_ == 128:
                    target[2 * (i0 + k) + qy, :, 0:128] = here.astype(BF)
                    target[2 * (i0 + k) + qy, :, 128:256] = right.astype(BF)
                else:
                    target[2 * (i0 + k) + qy, :, :] = jnp.where(lane_r < 64, here, right).astype(BF)

    def block_input(ref):
        def load(i0, g):
            lanes = ref.shape[2]
            rows = g * ref.shape[1]
            return [
                ref[pl.ds(i0, g)].reshape(rows, lanes),
                ref[pl.ds(i0 + 1, g)].reshape(rows, lanes),
            ]

        return load

    def layer(number, loads, first, count, g, wp, origin_y, origin_x, level, store):
        height, width = 32 >> level, 256 >> level
        low, high = edges(wp, origin_x, width)
        caps = (
            column_cap(number, 0, low, origin_x, width) if low else None,
            column_cap(number, high, wp - high, origin_x, width) if wp > high else None,
        )

        def step(it, _):
            i0 = first + it * g
            lhs = []
            for load in loads:
                lhs = lhs + load(i0, g)
            lhs = jnp.concatenate(lhs, axis=1) if len(lhs) > 1 else lhs[0]
            if number in FLIPPED:
                r = jnp.dot(lhs, c["w%d" % number][...], preferred_element_type=F32)
            else:
                r = nt(lhs, c["w%d" % number][...])
            if number in SPLIT:
                c["t128"][0 : g * wp, :] = r[:, 128:256]
                r = r[:, 0:128] + c["t128"][1 : g * wp + 1, :]
            store(finish(number, r, caps, i0, g, wp, origin_y, origin_x, height, width), i0)
            return 0

        for it in range(count):
            step(it, 0)

    def pool_into(pixels, number, wp):
        def store(pieces, i0):
            for k, piece in enumerate(pieces):
                pixels[i0 + k, 0:wp, :] = pooled(piece, NP[number])

        return store

    def windows(first, count, g):
        t = c["t128"]

        def step(it, _):
            i0 = first + it * g
            for k in range(g):
                rows = c["rows_yc"][pl.ds(2 * (i0 + k), 4)].reshape(64, 512)
                stacked = jnp.concatenate([rows[:, 0:256], rows[:, 256:512]], axis=0)
                turned = nt(c["eye"][...], stacked)
                c["fwin"][i0 + k, :, 0:128] = turned.astype(BF)
                t[k * 160 : (k + 1) * 160, :] = turned
            for k in range(g):
                c["fwin"][i0 + k, :, 128:256] = t[k * 160 + 1 : (k + 1) * 160 + 1, :].astype(BF)
            return 0

        for it in range(count):
            step(it, 0)

    def window_load(i0, g):
        return [c["fwin"][pl.ds(i0, g)].reshape(g * 160, 256)]

    def conv0(first, count, g):
        layer(0, [window_load], first, count, g, 160, -19, -35, 0, lambda p, i0: to_blocks(p, c["s1"], i0, 160, 128))

    def conv1(first, count, g):
        layer(1, [block_input(c["s1"])], first, count, g, 160, -18, -34, 0, pool_into(c["pix1"], 1, 160))

    def conv2(first, count, g):
        layer(2, [block_input(c["s2"])], first, count, g, 80, -8, -8, 1, pool_into(c["pix2"], 2, 80))

    windows(6, 2, 12)
    conv0(6, 2, 12)
    conv1(6, 2, 11)
    pack(c["pix1"], c["s2"], 3, 11, 80, 32, 0, 8)
    conv2(3, 1, 10)
    pack(c["pix2"], c["s3"], 0, 5, 48, 64, 3, 3)
    layer(3, [block_input(c["s3"])], 0, 1, 4, 48, 0, 0, 2, pool_into(c["pix3o"], 3, 48))

    lane8 = iota((8, 128), 1)
    pieces = []
    for half in range(2):
        for y in range(4):
            even = c["pix3o"][y, pl.ds(16 * half, 8, stride=2), :]
            odd = c["pix3o"][y, pl.ds(16 * half + 1, 8, stride=2), :]
            pieces.append(jnp.where(lane8 < 64, even, odd))
    c["tile_out"][...] = jnp.concatenate(pieces, axis=0).astype(BF)
    copies = []
    for number, (dy, dx) in enumerate(FAR):
        rows = pl.ds(0, 64) if dx == 0 else pl.ds(32, 32) if dx == 1 else pl.ds(0, 32)
        copy = pltpu.make_async_remote_copy(
            src_ref=c["tile_out"].at[rows],
            dst_ref=c["tiles_in"].at[number, rows],
            send_sem=send2.at[number],
            recv_sem=recv2.at[number],
            device_id=device(dy, dx),
            device_id_type=MESH,
        )
        copies.append((dy, dx, copy))

    wait = exchange(copies)

    windows(0, 1, 6)
    windows(30, 1, 5)
    conv0(0, 1, 6)
    conv0(30, 1, 5)
    conv1(0, 1, 6)
    conv1(28, 1, 6)
    pack(c["pix1"], c["s2"], 0, 3, 80, 32, 0, 8)
    pack(c["pix1"], c["s2"], 14, 3, 80, 32, 0, 8)
    conv2(0, 1, 3)
    conv2(13, 1, 3)
    pack(c["pix1"], c["k11"], 0, 12, 80, 32, 5, 13)
    pack(c["pix2"], c["k9"], 0, 8, 48, 64, 0, 0)

    wait()

    slot = {d: n for n, d in enumerate(FAR)}
    for ky in range(-3, 4):
        for kx in range(-1, 2):
            if (ky, kx) == (0, 0):
                tile = c["tile_out"][...].astype(F32)
            else:
                ok = (ty + ky >= 0) & (ty + ky < rows_ty) & (tx + kx >= 0) & (tx + kx < cols_tx)
                tile = jnp.where(jnp.where(ok, 1.0, 0.0) > 0, c["tiles_in"][slot[-ky, -kx]].astype(F32), 0.0)
            halves = (0, 1) if kx == 0 else (1,) if kx == -1 else (0,)
            for y in range(4):
                if ky == -3 and y < 3 or ky == 3 and y > 0:
                    continue
                for half in halves:
                    v = tile[32 * half + 8 * y : 32 * half + 8 * y + 8]
                    w = pltpu.roll(v, 64, 1)
                    row = 12 + 4 * ky + y
                    col = 32 * (kx + 1) + 16 * half
                    c["pix3"][row, pl.ds(col, 8, stride=2), :] = jnp.where(lane8 < 64, v, w)
                    c["pix3"][row, pl.ds(col + 1, 8, stride=2), :] = jnp.where(lane8 < 64, w, v)

    pack(c["pix3"], c["s4"], 0, 11, 32, 64, 3, 23)
    pack(c["pix3"], c["k7"], 0, 6, 32, 64, 8, 28)

    layer(4, [block_input(c["s4"])], 0, 1, 10, 32, -8, -8, 3, pool_into(c["pix4"], 4, 32))
    pack(c["pix4"], c["s5"], 0, 5, 16, 128, 0, 0)
    layer(5, [block_input(c["s5"])], 0, 1, 4, 16, -3, -3, 4, lambda p, i0: to_blocks(p, c["s6"], i0, 16, 512))
    layer(6, [block_input(c["s6"])], 0, 1, 3, 16, -2, -2, 4, lambda p, i0: to_pixels(p, c["r7"], i0, 16, 32, 128))
    layer(
        7, [block_input(c["r7"]), block_input(c["k7"])], 0, 1, 5, 32, -3, -3, 3,
        lambda p, i0: to_blocks(p, c["s8"], i0, 32, 512),
    )
    layer(8, [block_input(c["s8"])], 0, 1, 4, 32, -2, -2, 3, lambda p, i0: to_pixels(p, c["r9"], i0, 32, 48, 128))
    layer(
        9, [block_input(c["r9"]), block_input(c["k9"])], 0, 1, 7, 48, -3, -3, 2,
        lambda p, i0: to_blocks(p, c["s10"], i0, 48, 512),
    )
    layer(10, [block_input(c["s10"])], 0, 1, 6, 48, -2, -2, 2, lambda p, i0: to_pixels(p, c["r11"], i0, 48, 80, 128))
    layer(
        11, [block_input(c["r11"]), block_input(c["k11"])], 0, 1, 11, 80, -3, -3, 1,
        lambda p, i0: to_blocks(p, c["s12"], i0, 80, 256),
    )
    layer(12, [block_input(c["s12"])], 0, 1, 10, 80, -2, -2, 1, lambda p, i0: to_pixels(p, c["r13"], i0, 80, 144, 64))

    def features_load(i0, g):
        return [c["fwin"][pl.ds(i0 + 8, g), 16:160, :].reshape(g * 144, 256)]

    layer(
        13, [block_input(c["r13"]), features_load], 0, 1, 10, 144, -3, -3, 0,
        lambda p, i0: to_blocks(p, c["s14"], i0, 144, 256),
    )
    layer(
        13, [block_input(c["r13"]), features_load], 10, 1, 9, 144, -3, -3, 0,
        lambda p, i0: to_blocks(p, c["s14"], i0, 144, 256),
    )
    layer(14, [block_input(c["s14"])], 0, 2, 9, 144, -2, -2, 0, lambda p, i0: to_blocks(p, c["s15"], i0, 144, 128))

    lane144 = iota((16, 144), 1)

    def last(i, _):
        field = jnp.concatenate([c["s15"][i], c["s15"][i + 1]], axis=1)
        r = nt(c["w15"][...], field)
        r = r[0:16] + pltpu.roll(r[16:32], 143, 1) + c["column"][...]
        r = jnp.where(lane144 < 129, r, 0.0)
        c["z0"][pl.ds(pl.multiple_of(8 * i, 8), 8), :] = r[0:8]
        c["z1"][pl.ds(pl.multiple_of(8 * i, 8), 8), :] = r[8:16]
        return 0

    c["z0"][136:144, :] = jnp.zeros((8, 144), F32)
    c["z1"][136:144, :] = jnp.zeros((8, 144), F32)
    lax.fori_loop(0, 17, last, 0, unroll=17)
    at = iota((144, 256), 1) - 2 * iota((144, 256), 0)
    even = (at == -1).astype(F32).astype(BF)
    odd = (at == 0).astype(F32).astype(BF)
    wide = jnp.dot(c["z0"][...].astype(BF), even, preferred_element_type=F32) + jnp.dot(
        c["z1"][...].astype(BF), odd, preferred_element_type=F32
    )
    for half in range(2):
        lanes = slice(128 * half, 128 * half + 128)
        c["zf"][half] = wide[:, lanes]
        for o in range(3):
            c["out32"][2 * o + half, pl.ds(0, 16, stride=2), :] = c["zf"][half, pl.ds(3 + o, 16, stride=8), :]
            c["out32"][2 * o + half, pl.ds(1, 16, stride=2), :] = c["zf"][half, pl.ds(8 + o, 16, stride=8), :]
            out[o, :, lanes] = c["out32"][2 * o + half].astype(BF)


def body(sizes, features, *rest):
    weights, biases = list(rest[:16]), rest[16]
    for number in FLIPPED:
        weights[number] = jnp.transpose(weights[number], (0, 1, 3, 2) if number else (0, 3, 1, 2))
    vmem = pl.BlockSpec(memory_space=pltpu.VMEM)
    scratch = [pltpu.VMEM(shape, kind) for shape, kind in SCRATCH.values()]
    scratch += [pltpu.SemaphoreType.DMA((n,)) for n in (8, 8, 20, 20)]
    scratch += [pltpu.VMEM(w.shape, BF) for w in weights] + [pltpu.SemaphoreType.DMA((16,))]
    return pl.pallas_call(
        functools.partial(kernel, sizes),
        out_shape=jax.ShapeDtypeStruct((3, 32, 256), BF),
        in_specs=[vmem] + [pl.BlockSpec(memory_space=pl.ANY)] * 16 + [vmem],
        out_specs=vmem,
        scratch_shapes=scratch,
        compiler_params=pltpu.CompilerParams(
            collective_id=0, has_side_effects=True, vmem_limit_bytes=58 << 20
        ),
    )(features, *weights, biases)


def solution(mesh):
    sizes = (mesh.shape["ty"], mesh.shape["tx"])
    return jax.shard_map(
        functools.partial(body, sizes),
        mesh=mesh,
        in_specs=(P(None, "ty", "tx"),) + (P(),) * 17,
        out_specs=P(None, "ty", "tx"),
        check_vma=False,
    )
```
